128 devices in a mesh: label: 16 (over z, y_lo, core), dp: 8 (over y_hi, x).
Axes of the slice: x: 4, y: 4 (y_hi: 2, y_lo: 2; y = y_hi * 2 + y_lo), z: 4, core: 2. Of those that a mesh axis runs over, the one named last changes fastest.
Arguments:
- hidden_in: bfloat16 [16384, 768], P(('dp', 'label')), may hold values from -6 to 6
- norm_gain: float32 [768], replicated, may hold values from 0.25 to 1.75
- w_in: bfloat16 [768, 3072], replicated, may hold values from -0.21875 to 0.21875
- w_out: bfloat16 [3072, 768], replicated, may hold values from -0.15625 to 0.15625
- classifier: bfloat16 [32768, 768], P('label'), may hold values from -0.21875 to 0.21875
- centroids: bfloat16 [512, 768], P('label'), may hold values from -0.21875 to 0.21875
- radii: float32 [512], P('label'), may hold values from 0.005 to 0.08
- shortlist: int32 [16384, 16], P('dp'), may hold values from 0 to 511, all different within a row; in each aligned block of 2048 rows (0 to 2047, 2048 to 4095, ...) at most 80 rows name the same one
- positives: int32 [16384, 4], P('dp'), may hold values from 0 to 1023
- block_slot: int32 [512], replicated, may hold values from 0 to 511, each once
Outputs:
- bound_top: float32 [16384], P('dp')
- loss: float32 [16384], P(('dp', 'label'))
- query_grad: bfloat16 [16384, 768], P(('dp', 'label'))
- class_grad: bfloat16 [32768, 768], P(('label', 'dp'))
The draws below stay inside these ranges and needn't reach their ends.
Inputs may be any that keep to these rules, and one draw needn't show every extreme that they name: `shortlist`: each query names 16 different blocks; among the 2048 queries of each data group no block is named by more than 80 queries, and some block by exactly 80; every block is named somewhere. `block_slot`: each slot once.
All inputs are finite; a program needn't handle non-finite values.
Results may differ from the reference program's by a relative error of at most 0.019.
Values may be sent and summed in bfloat16 or wider, within the bound.
No kernel may reach another device: no remote copies, remote signals or barrier semaphores. Data moves between devices by JAX's collectives and lax.ppermute only.
A program may use at most 128 MiB of HBM per device.

```python
import math
import jax
import jax.numpy as jnp
import numpy as np
from jax import lax

D = 768
FF = 3072
BL = 64
LBLK = 32
K = 16
QCAP = 80
P_SIZE = 4
QG = 2048
QUERIES = 16384
BLOCKS = 512
LABELS = 32768
N_LABEL = 16
N_DP = 8


def touch_ends(drawn, stream_key, smallest, top_value):
    index_at = [jax.random.randint(jax.random.fold_in(stream_key, axis), (), 0, length) for axis, length in enumerate(drawn.shape)]
    widest = drawn.shape.index(max(drawn.shape))
    neighbour = index_at[:widest] + [(index_at[widest] + 1) % drawn.shape[widest]] + index_at[widest + 1:]
    return drawn.at[tuple(index_at)].set(smallest).at[tuple(neighbour)].set(top_value)


def shard_levels(key, extent, split, low, high):
    gain = 1.0
    for dim, blocks in split:
        steps = jax.random.uniform(jax.random.fold_in(jax.random.fold_in(key, 6), dim), (blocks,), jnp.float32, low / len(split), high / len(split))
        gain = gain * jnp.repeat(jnp.exp(steps), extent[dim] // blocks).reshape((-1,) + (1,) * (len(extent) - 1 - dim))
    return gain


def routed_block(rng, own, number, rows, number_of, top, most, slope):
    ranking = jax.random.permutation(rng, number_of)
    packed, ordinary = shares(number_of, rows * top, most, slope, True), shares(number_of, rows * top, most, slope, False)
    places = jnp.arange(number_of)

    def named(sizes, rotation):
        used = int((sizes > 0).sum())
        fixed = max(1, used // 4)
        passed = fixed + (places - fixed + rotation * (used - fixed)) % max(1, number_of - fixed)
        return jnp.zeros((number_of,), jnp.int32).at[ranking[jnp.where(places < fixed, places, passed)]].set(jnp.asarray(sizes, jnp.int32))

    sizes = jnp.where(number % 4 == 0, named(packed, number // 4), named(ordinary, number - number // 4 - 1))
    mixed = jax.random.permutation(jax.random.fold_in(own, 3), number_of)
    source_of, receiver = mixed[0:number_of // 2 * 2:2], mixed[1:number_of // 2 * 2:2]
    room = jnp.minimum(sizes[source_of] - 1, most - sizes[receiver]) // 2
    room = jnp.where((source_of == ranking[0]) | (receiver == ranking[0]) | (sizes[receiver] == 0), 0, jnp.maximum(room, 0))
    passed = jax.random.randint(jax.random.fold_in(own, 4), (number_of // 2,), 0, 1 << 20) % (room + 1)
    sizes = sizes.at[source_of].add(-passed).at[receiver].add(passed)
    labels = jnp.searchsorted(jnp.cumsum(sizes), jnp.arange(rows * top), side="right").astype(jnp.int32)
    table = labels.reshape(top, rows).T
    table = table[jax.random.permutation(jax.random.fold_in(own, 1), rows)]
    rotation = jax.random.randint(jax.random.fold_in(own, 2), (rows, 1), 0, top)
    return jnp.take_along_axis(table, (jnp.arange(top)[None, :] + rotation) % top, axis=1)


def shares(amount, total, reach, lean, full):
    loads = [(1 << 20) // math.isqrt(rank ** lean) + 1 for rank in range(1, amount + 1)]
    largest = reach if full else min(reach, max(-(-total // amount), total * loads[0] // sum(loads)))
    least = 1 if total - largest >= amount - 1 else 0
    counts, rest = [largest] + [least] * (amount - 1), total - largest - least * (amount - 1)
    while rest > 0:
        candidates = [i for i in range(1, amount) if counts[i] < largest] or [i for i in range(1, amount) if counts[i] < reach]
        pool, remaining = sum([loads[i] for i in candidates]), rest
        for i in candidates:
            extra = min(reach - counts[i], max(1, remaining * loads[i] // pool), rest)
            counts[i] = counts[i] + extra
            rest = rest - extra
    return np.array(counts)


def gaussian(rng, shape, spread, limit, pieces=(), kind=jnp.bfloat16):
    loudness = shard_levels(rng, shape, pieces, -0.22, 0.18) if pieces else 1.0
    array = jax.random.normal(rng, shape, jnp.float32) * spread * loudness
    return jnp.minimum(jnp.maximum(array, -limit), limit).astype(kind)


def setup_inputs(seed: int = 0) -> dict:
    splits = jax.random.split(jax.random.key(seed), 11)
    hidden_in = gaussian(splits[0], (QUERIES, D), 1.0, 6.0, ((0, 128),))
    norm_gain = jnp.clip(1.0 + 0.15 * jax.random.normal(splits[1], (D,), jnp.float32), 0.25, 1.75)
    w_in = gaussian(splits[2], (D, FF), D ** -0.5, 0.21875)
    w_out = gaussian(splits[3], (FF, D), (FF // 2) ** -0.5, 0.15625)
    classifier = gaussian(splits[4], (LABELS, D), D ** -0.5, 0.21875, ((0, 16),))
    centroids = gaussian(splits[5], (BLOCKS, D), D ** -0.5, 0.21875, ((0, 16),))
    radii = jnp.clip(jnp.exp(math.log(0.08) - 2.7725887 * jax.random.uniform(splits[6], (BLOCKS,), jnp.float32) ** shard_levels(splits[6], (BLOCKS,), ((0, 16),), -0.2, 0.2)), 0.005, 0.08)
    shortlist_keys = jax.random.split(jax.random.fold_in(splits[7], 1), QUERIES // QG)
    shortlist_turns = jax.random.permutation(jax.random.fold_in(splits[7], 3), QUERIES // QG)
    shortlist = jax.vmap(lambda own, number: routed_block(jax.random.fold_in(splits[7], 2), own, number, QG, BLOCKS, K, QCAP, 2))(shortlist_keys, shortlist_turns).reshape((QUERIES, K))
    positives = touch_ends(jax.random.randint(splits[8], (QUERIES, P_SIZE), 0, K * BL), jax.random.fold_in(splits[8], 1), 0, (K * BL) - 1).astype(jnp.int32)
    block_slot = jax.random.permutation(splits[9], BLOCKS).astype(jnp.int32)
    return {"hidden_in": hidden_in, "norm_gain": norm_gain, "w_in": w_in, "w_out": w_out, "classifier": classifier, "centroids": centroids, "radii": radii, "shortlist": shortlist, "positives": positives, "block_slot": block_slot}


def encode(hidden_in, norm_gain, w_in, w_out):
    values = hidden_in.astype(jnp.float32)
    meansq = lax.optimization_barrier(jnp.mean(values * values, axis=-1, keepdims=True))
    normed = (values * lax.rsqrt(meansq + 1e-06) * norm_gain).astype(jnp.bfloat16)
    active = jax.nn.gelu(jnp.dot(normed, w_in, preferred_element_type=jnp.float32), approximate=True).astype(jnp.bfloat16)
    return (values + jnp.dot(active, w_out, preferred_element_type=jnp.float32)).astype(jnp.bfloat16)

def group_terms(encoded, shortlist, positives, classifier, block_slot):
    total = QG * K
    slots = block_slot[shortlist].reshape(-1).astype(jnp.int32)
    order = jnp.argsort(slots, stable=True).astype(jnp.int32)
    sorted_slots = slots[order]
    every = jnp.arange(BLOCKS, dtype=jnp.int32)
    first = jnp.searchsorted(sorted_slots, every, side='left').astype(jnp.int32)
    last = jnp.searchsorted(sorted_slots, every, side='right').astype(jnp.int32)
    offsets = jnp.arange(QCAP, dtype=jnp.int32)
    valid_flags = offsets[None, :] < (last - first)[:, None]
    pairs = order[jnp.minimum(first[:, None] + offsets[None, :], total - 1)]
    rows = (pairs // K).reshape(N_LABEL, LBLK, QCAP)
    which = (pairs % K).reshape(N_LABEL, LBLK, QCAP)
    valid_flags = valid_flags.reshape(N_LABEL, LBLK, QCAP)
    label_weights = classifier.reshape(N_LABEL, LBLK, BL, D)
    inner = jnp.arange(BL, dtype=jnp.int32)

    def step(carry, items):
        grads, losses = carry
        rows_c, which_c, valid_column, weight_c = items
        chosen_labels = encoded[rows_c].astype(jnp.float32)
        weight_float = weight_c.astype(jnp.float32)
        label_logits = jnp.einsum('mrc,mnc->mrn', chosen_labels, weight_float)
        wanted = which_c[:, :, None] * BL + inner[None, None, :]
        posv = positives[rows_c]
        target_labels = jnp.zeros(wanted.shape, jnp.float32)
        for index_p in range(P_SIZE):
            target_labels = jnp.maximum(target_labels, (posv[:, :, index_p][:, :, None] == wanted).astype(jnp.float32))
        valid_mask = valid_column.astype(jnp.float32)[:, :, None]
        shortlist_entry = lax.optimization_barrier(jnp.sum((jax.nn.softplus(label_logits) - target_labels * label_logits) * valid_mask, axis=-1))
        logit_slope = ((jax.nn.sigmoid(label_logits) - target_labels) * valid_mask).astype(jnp.bfloat16).astype(jnp.float32)
        backward_signal = jnp.einsum('zir,zrk->zik', logit_slope, weight_float)
        weight_gradient = jnp.einsum('wzv,wzc->wvc', logit_slope, chosen_labels)
        flat = rows_c.reshape(-1)
        partial_grad = jnp.zeros((QG, D), jnp.float32).at[flat].add(backward_signal.reshape(-1, D))
        rounded = lax.optimization_barrier(partial_grad.astype(jnp.bfloat16))
        grads = grads + rounded.astype(jnp.float32)
        losses = losses.at[flat].add(shortlist_entry.reshape(-1))
        return ((grads, losses), weight_gradient.astype(jnp.bfloat16))
    start = (jnp.zeros((QG, D), jnp.float32), jnp.zeros((QG,), jnp.float32))
    (grads, losses), wparts = lax.scan(step, start, (rows, which, valid_flags, label_weights))
    return (grads, losses, wparts.reshape(LABELS, D))

def reference(hidden_in, norm_gain, w_in, w_out, classifier, centroids, radii, shortlist, positives, block_slot):
    encoded = encode(hidden_in, norm_gain, w_in, w_out)

    def bound_rows(block):
        values = block.astype(jnp.float32)
        norms = jnp.sqrt(lax.optimization_barrier(jnp.sum(values * values, axis=-1)))
        scores = jnp.dot(block, centroids.T, preferred_element_type=jnp.float32) + norms[:, None] * radii[None, :]
        return lax.optimization_barrier(jnp.max(scores, axis=-1))
    bound_top = lax.map(bound_rows, encoded.reshape(N_DP, QG, D)).reshape(QUERIES)
    grad_list = []
    loss_list = []
    class_total = jnp.zeros((LABELS, D), jnp.float32)
    for group in range(N_DP):
        low = group * QG
        grads, losses, wpart = group_terms(encoded[low:low + QG], shortlist[low:low + QG], positives[low:low + QG], classifier, block_slot)
        grad_list.append(grads)
        loss_list.append(losses)
        class_total = class_total + wpart.astype(jnp.float32)
    query_grad = jnp.concatenate(grad_list, axis=0).astype(jnp.bfloat16)
    loss = jnp.concatenate(loss_list, axis=0)
    return (bound_top, loss, query_grad, class_total.astype(jnp.bfloat16))
```

```python
import functools

import jax
import jax.numpy as jnp
from jax import lax
from jax.experimental import pallas as pl
from jax.experimental.pallas import tpu as pltpu
from jax.sharding import PartitionSpec as P

F32 = jnp.float32
BF16 = jnp.bfloat16

NZ, NY, NC = 4, 2, 2
NX, NYH = 4, 2
ROWS = 128
PLANE = ROWS * NY * NC
EXTRA = 16
D = 768
BL = 64
K = 16
P_SIZE = 4
LBLK = 32
LOCAL = LBLK * BL
BLOCKS = 512
TILE = 512
SLOTS = TILE // BL
CROWS = 48
OUTSIDE = -1e30
MIB = 1024 * 1024

DP_ORDER = ((2, 1), (1, 1), (3, 1), (2, 0), (1, 0), (3, 0), (0, 1), (0, 0))


def label_perm(dz, dy, dc):
    at = lambda z, y, c: (z % NZ) * 4 + (y % NY) * 2 + c % NC
    return [
        (at(z, y, c), at(z + dz, y + dy, c + dc))
        for z in range(NZ)
        for y in range(NY)
        for c in range(NC)
    ]


def dp_perm(dx, dy):
    at = lambda x, y: (y % NYH) * 4 + x % NX
    return [(at(x, y), at(x + dx, y + dy)) for y in range(NYH) for x in range(NX)]


def send_label(x, dz, dy, dc):
    return lax.ppermute(x, "label", label_perm(dz, dy, dc))


def vmem(*shape):
    return pl.BlockSpec(memory_space=pltpu.VMEM)


def params(limit=48):
    return pltpu.CompilerParams(vmem_limit_bytes=limit * MIB)


def cost(us):
    return pl.CostEstimate(flops=int(us * 8e8), bytes_accessed=int(us * 1e5), transcendentals=0)


def encode(hidden_in, norm_gain, w_in, w_out):
    values = hidden_in.astype(F32)
    meansq = jnp.mean(values * values, axis=-1, keepdims=True)
    normed = (values * lax.rsqrt(meansq + 1e-06) * norm_gain).astype(BF16)
    active = jax.nn.gelu(
        jnp.dot(normed, w_in, preferred_element_type=F32), approximate=True
    ).astype(BF16)
    return (values + jnp.dot(active, w_out, preferred_element_type=F32)).astype(BF16)


def prepare_kernel(me_ref, sl_ref, pos_ref, bs_ref, neg_ref, wa_ref, wb_ref):
    me = me_ref[0]
    z, low = me // 4, me % 4
    slot_rows = lax.broadcasted_iota(jnp.int32, (LBLK, BLOCKS), 0) + me * LBLK
    ids = lax.broadcasted_iota(jnp.int32, (LBLK, BLOCKS), 1).astype(F32)
    here = jnp.sum(jnp.where(bs_ref[...] == slot_rows, ids, 0.0), axis=1, keepdims=True)
    here = jnp.broadcast_to(here, (LBLK, ROWS))
    which = lax.broadcasted_iota(jnp.int32, (K, ROWS), 0)
    for dz in range(NZ):
        for j in range(4):
            nat = lax.rem(z + NZ - dz, NZ) * 4 + (low ^ j)
            lanes = pl.ds(pl.multiple_of(nat * ROWS, ROWS), ROWS)
            sl = sl_ref[:, lanes].astype(F32)
            pos = pos_ref[:, lanes]
            neg = jnp.full((LBLK, ROWS), OUTSIDE, F32)
            for k in range(K):
                neg = jnp.where(here == sl[k : k + 1], 0.0, neg)
            wa = jnp.zeros((LBLK, ROWS), jnp.int32)
            wb = jnp.zeros((LBLK, ROWS), jnp.int32)
            for p in range(P_SIZE):
                kp, jp = pos[p : p + 1] >> 6, pos[p : p + 1] & 63
                bid = jnp.sum(jnp.where(which == kp, sl, 0.0), axis=0, keepdims=True)
                bit = jnp.full((1, ROWS), 1, jnp.int32) << (31 - (jp & 31))
                match = here == bid
                wa = wa | jnp.where(match, jnp.where(jp < 32, bit, 0), 0)
                wb = wb | jnp.where(match, jnp.where(jp < 32, 0, bit), 0)
            out = pl.ds(j * ROWS, ROWS)
            neg_ref[dz, :, out] = neg
            wa_ref[dz, :, out] = wa
            wb_ref[dz, :, out] = wb


def prepare(me, sl, pos, bs):
    out = lambda t: jax.ShapeDtypeStruct((NZ, LBLK, PLANE), t)
    return pl.pallas_call(
        prepare_kernel,
        out_shape=(out(F32), out(jnp.int32), out(jnp.int32)),
        in_specs=[pl.BlockSpec(memory_space=pltpu.SMEM), vmem(), vmem(), vmem()],
        out_specs=(vmem(), vmem(), vmem()),
        compiler_params=params(),
        cost_estimate=cost(3),
        name="prepare",
    )(me, sl, pos, bs)


def split3(value):
    hi = value.astype(BF16)
    rest = value - hi.astype(F32)
    mid = rest.astype(BF16)
    lo = (rest - mid.astype(F32)).astype(BF16)
    return hi, mid, lo


def loss_rows(row):
    hi, mid, lo = split3(row)
    return jnp.concatenate([hi, mid, lo, jnp.zeros((EXTRA, D - 3 * ROWS), BF16)], axis=1)


def joined(rows):
    return rows[:, :ROWS] + rows[:, ROWS : 2 * ROWS] + rows[:, 2 * ROWS : 3 * ROWS]


def slope_kernel(q0, q1, q2, q3, c_ref, neg_ref, wa_ref, wb_ref, s_ref, a0_ref, a1_ref,
                 q_ref, x_ref, acc_ref, loss_ref):
    i = pl.program_id(0)

    @pl.when(i == 0)
    def _():
        for j, q in enumerate((q0, q1, q2, q3)):
            q_ref[j * ROWS : (j + 1) * ROWS, :] = q[...]
        acc_ref[...] = jnp.zeros_like(acc_ref)
        loss_ref[...] = jnp.zeros_like(loss_ref)

    x_ref[...] = lax.dot_general(
        c_ref[...], q_ref[...], (((1,), (1,)), ((), ())), preferred_element_type=F32
    )
    shift = lax.broadcasted_iota(jnp.int32, (32, ROWS), 0)
    for t in range(PLANE // ROWS):
        lanes = slice(t * ROWS, (t + 1) * ROWS)
        prod = jnp.ones((8, ROWS), F32)
        relu = jnp.zeros((8, ROWS), F32)
        for s in range(SLOTS):
            rows = slice(s * BL, (s + 1) * BL)
            x = x_ref[rows, lanes] + neg_ref[s : s + 1, lanes]
            bits = jnp.concatenate(
                [wa_ref[s : s + 1, lanes] << shift, wb_ref[s : s + 1, lanes] << shift], axis=0
            )
            hit = bits < 0
            flipped = -x
            e = jnp.exp(jnp.minimum(x, flipped))
            x = jnp.where(hit, flipped, x)
            u = 1.0 + e
            sig = jnp.where(x >= 0.0, 1.0, e) * pl.reciprocal(u, approx=True)
            s_ref[rows, lanes] = jnp.where(hit, -sig, sig).astype(BF16)
            u8 = u.reshape(8, 8, ROWS)
            r8 = jnp.maximum(x, 0.0).reshape(8, 8, ROWS)
            for n in range(8):
                prod = prod * u8[n]
                relu = relu + r8[n]
        loss_ref[:, lanes] += jnp.log(prod) + relu
    acc_ref[...] += lax.dot_general(
        s_ref[...], c_ref[...], (((0,), (0,)), ((), ())), preferred_element_type=F32
    )

    @pl.when(i == pl.num_programs(0) - 1)
    def _():
        for j in range(4):
            out, dy = (a0_ref, a1_ref)[j % 2], j // 2
            rows = slice(j * ROWS, (j + 1) * ROWS)
            out[dy, :ROWS, :] = acc_ref[rows, :].astype(BF16)
            row = jnp.sum(loss_ref[:, rows], axis=0, keepdims=True)
            out[dy, ROWS:, :] = loss_rows(jnp.broadcast_to(row, (EXTRA, ROWS)))


def slopes(plane, shards, classifier, neg, wa, wb):
    whole = pl.BlockSpec((ROWS, D), lambda i: (0, 0))
    flag = pl.BlockSpec((None, SLOTS, PLANE), lambda i: (plane, i, 0))
    part = jax.ShapeDtypeStruct((NY, ROWS + EXTRA, D), BF16)
    part_spec = pl.BlockSpec((NY, ROWS + EXTRA, D), lambda i: (0, 0, 0))
    return pl.pallas_call(
        slope_kernel,
        out_shape=(jax.ShapeDtypeStruct((LOCAL, PLANE), BF16), part, part),
        grid=(LOCAL // TILE,),
        in_specs=[whole] * 4 + [pl.BlockSpec((TILE, D), lambda i: (i, 0)), flag, flag, flag],
        out_specs=(pl.BlockSpec((TILE, PLANE), lambda i: (i, 0)), part_spec, part_spec),
        scratch_shapes=[
            pltpu.VMEM((PLANE, D), BF16),
            pltpu.VMEM((TILE, PLANE), F32),
            pltpu.VMEM((PLANE, D), F32),
            pltpu.VMEM((8, PLANE), F32),
        ],
        compiler_params=params(),
        cost_estimate=cost(7),
        name="slopes",
    )(*shards, classifier, neg, wa, wb)


def pair_kernel(a_ref, b_ref, out_ref):
    for dy in range(NY):
        out_ref[dy, :ROWS, :] = (
            a_ref[dy, :ROWS, :].astype(F32) + b_ref[dy, :ROWS, :].astype(F32)
        ).astype(BF16)
        out_ref[dy, ROWS:, :] = loss_rows(
            joined(a_ref[dy, ROWS:, :].astype(F32) + b_ref[dy, ROWS:, :].astype(F32))
        )


def pair(a, b):
    return pl.pallas_call(
        pair_kernel,
        out_shape=jax.ShapeDtypeStruct(a.shape, BF16),
        in_specs=[vmem(), vmem()],
        out_specs=vmem(),
        compiler_params=params(16),
        cost_estimate=cost(1),
        name="pair",
    )(a, b)


def across_kernel(a, b, c, d, out_ref):
    total = sum(r[1].astype(F32) for r in (a, b, c, d))
    out_ref[:ROWS, :] = total[:ROWS].astype(BF16)
    out_ref[ROWS:, :] = loss_rows(joined(total[ROWS:]))


def across(parts):
    return pl.pallas_call(
        across_kernel,
        out_shape=jax.ShapeDtypeStruct((ROWS + EXTRA, D), BF16),
        in_specs=[vmem()] * 4,
        out_specs=vmem(),
        compiler_params=params(16),
        cost_estimate=cost(1),
        name="across",
    )(*parts)


def finish_kernel(a, b, c, d, y_ref, grad_ref, loss_ref):
    total = sum(r[0].astype(F32) for r in (a, b, c, d)) + y_ref[...].astype(F32)
    grad_ref[...] = total[:ROWS].astype(BF16)
    loss_ref[...] = joined(total[ROWS : ROWS + 8])[:1]


def finish(parts, y):
    return pl.pallas_call(
        finish_kernel,
        out_shape=(
            jax.ShapeDtypeStruct((ROWS, D), BF16),
            jax.ShapeDtypeStruct((1, ROWS), F32),
        ),
        in_specs=[vmem()] * 5,
        out_specs=(vmem(), vmem()),
        compiler_params=params(16),
        cost_estimate=cost(1),
        name="finish",
    )(*parts, y)


def class_kernel(count, order_ref, *refs):
    s_refs, q_refs = refs[:NZ], refs[NZ : NZ + 16]
    outs, q_ref = refs[NZ + 16 : NZ + 16 + count], refs[-1]
    i = pl.program_id(0)

    @pl.when(i == 0)
    def _():
        for r, q in enumerate(q_refs):
            q_ref[r * ROWS : (r + 1) * ROWS, :] = q[...]

    total = sum(
        jnp.dot(
            s[...], q_ref[n * PLANE : (n + 1) * PLANE, :], preferred_element_type=F32
        )
        for n, s in enumerate(s_refs)
    ).astype(BF16)
    for n, out in enumerate(outs):

        @pl.when(i == n)
        def _():
            out[...] = total


def class_blocks(order, slope_planes, shards):
    count = order.shape[0]
    rows = LOCAL // (NX * NYH)
    return pl.pallas_call(
        functools.partial(class_kernel, count),
        out_shape=[jax.ShapeDtypeStruct((rows, D), BF16)] * count,
        grid_spec=pltpu.PrefetchScalarGridSpec(
            num_scalar_prefetch=1,
            grid=(count,),
            in_specs=[pl.BlockSpec((rows, PLANE), lambda i, o: (o[i], 0))] * NZ
            + [pl.BlockSpec((ROWS, D), lambda i, o: (0, 0))] * 16,
            out_specs=[pl.BlockSpec((rows, D), lambda i, o: (0, 0))] * count,
            scratch_shapes=[pltpu.VMEM((16 * ROWS, D), BF16)],
        ),
        compiler_params=params(),
        cost_estimate=cost(5),
        name="class_blocks",
    )(order, *slope_planes, *shards)


def bound_kernel(me_ref, cent_ref, radii_ref, *refs):
    q_refs, out_ref = refs[:16], refs[16]
    me = me_ref[0]
    for r, q in enumerate(q_refs):
        value = q[...].astype(F32)
        norm = jnp.sqrt(jnp.sum(value * value, axis=1, keepdims=True))
        score = lax.dot_general(
            q[...], cent_ref[...], (((1,), (1,)), ((), ())), preferred_element_type=F32
        )
        top = jnp.max(score + norm * radii_ref[...], axis=1, keepdims=True)
        row = jnp.broadcast_to(top, (ROWS, ROWS)).T[:1]
        nat = lax.rem(me // 4 + NZ - r // 4, NZ) * 4 + ((me % 4) ^ (r % 4))
        out_ref[:, pl.ds(pl.multiple_of(nat * ROWS, ROWS), ROWS)] = row


def bounds(me, cent, radii, shards):
    return pl.pallas_call(
        bound_kernel,
        out_shape=jax.ShapeDtypeStruct((1, 16 * ROWS), F32),
        in_specs=[pl.BlockSpec(memory_space=pltpu.SMEM)] + [vmem()] * 18,
        out_specs=vmem(),
        compiler_params=params(),
        cost_estimate=cost(4),
        name="bounds",
    )(me, cent, radii, *shards)


def on_device(
    hidden_in,
    norm_gain,
    w_in,
    w_out,
    classifier,
    centroids,
    radii,
    shortlist,
    positives,
    block_slot,
):
    label = lax.axis_index("label")
    dp = lax.axis_index("dp")
    me = label.astype(jnp.int32).reshape(1)

    hi = lax.reduce_precision(radii, 8, 7)
    mid = lax.reduce_precision(radii - hi, 8, 7)
    lo = lax.reduce_precision(radii - hi - mid, 8, 7)
    terms = jnp.stack([hi, mid, lo]).astype(BF16)
    packed = jnp.concatenate(
        [centroids, jnp.pad(terms, ((0, CROWS - LBLK - 3), (0, D - LBLK)))], axis=0
    )
    every = lax.all_gather(packed, "label", axis=0)

    neg, wa, wb = prepare(me, shortlist.T, positives.T, block_slot.reshape(1, -1))
    encoded = encode(hidden_in, norm_gain, w_in, w_out)

    held = {(0, 0, 0): encoded, (0, 1, 0): send_label(encoded, 0, 1, 0)}
    for dz in (2, 1, 3):
        held[dz, 0, 0] = send_label(encoded, dz, 0, 0)
    for dz in (2, 1, 3):
        held[dz, 1, 0] = send_label(held[0, 1, 0], dz, 0, 0)
    for dz in range(NZ):
        for dy in range(NY):
            held[dz, dy, 1] = send_label(held[dz, dy, 0], 0, 0, 1)
    planes = [[held[dz, dy, dc] for dy in range(NY) for dc in range(NC)] for dz in range(NZ)]
    shards = [q for plane in planes for q in plane]

    slope_planes = [None] * NZ
    parts = [None] * NZ
    for dz in (0, 1, 3, 2):
        slope_planes[dz], keep, give = slopes(dz, planes[dz], classifier, neg, wa, wb)
        both = pair(keep, send_label(give, 0, 0, 1))
        parts[dz] = both if dz == 0 else send_label(both, -dz, 0, 0)

    order = jnp.stack(
        [((dp // NX + dy) % NYH) * NX + (dp % NX + dx) % NX for dx, dy in DP_ORDER]
    ).astype(jnp.int32)
    blocks = class_blocks(order[:4], slope_planes, shards)
    blocks = blocks + class_blocks(order[4:], slope_planes, shards)
    class_total = blocks[-1].astype(F32)
    for (dx, dy), block in zip(DP_ORDER[:-1], blocks):
        class_total = class_total + lax.ppermute(block, "dp", dp_perm(dx, dy)).astype(F32)

    query_grad, loss = finish(parts, send_label(across(parts), 0, 1, 0))

    cent = every[:, :LBLK].reshape(BLOCKS, D)
    pieces = every[:, LBLK : LBLK + 3, :LBLK].astype(F32)
    radius = (pieces[:, 0] + pieces[:, 1] + pieces[:, 2]).reshape(1, BLOCKS)
    bound_top = bounds(me, cent, radius, shards)
    return (
        bound_top.reshape(-1),
        loss.reshape(-1),
        query_grad,
        class_total.astype(BF16),
    )


def solution(mesh):
    placed = (
        P(("dp", "label"), None),
        P(),
        P(),
        P(),
        P("label", None),
        P("label", None),
        P("label"),
        P("dp", None),
        P("dp", None),
        P(),
    )
    return jax.shard_map(
        on_device,
        mesh=mesh,
        in_specs=placed,
        out_specs=(P("dp"), P(("dp", "label")), P(("dp", "label"), None), P(("label", "dp"), None)),
        check_vma=False,
    )
```

```python
import functools

import jax
import jax.numpy as jnp
from jax import lax
from jax.experimental import pallas as pl
from jax.experimental.pallas import tpu as pltpu
from jax.sharding import PartitionSpec as P

F32 = jnp.float32
BF16 = jnp.bfloat16

NZ, NY = 4, 2
NX, NYH = 4, 2
ROWS = 128
PAIR = 2 * ROWS
PAIRS = 8
EXTRA = 16
D = 768
FF = 3072
FTILE = 1024
BL = 64
K = 16
P_SIZE = 4
LBLK = 32
LOCAL = LBLK * BL
BLOCKS = 512
TILE = 256
CROWS = 48
LN2 = 0.6931471805599453
MIB = 1024 * 1024

SOURCE = (
    ((0, 0), (0, 0)),
    ((-1, 0), (1, 0)),
    ((1, 0), (-1, 0)),
    ((0, 1), (2, 0)),
    ((2, 0), (0, 1)),
    ((-1, 1), (1, 1)),
    ((1, 1), (-1, 1)),
    ((2, 1), (2, 1)),
)

DP_ORDER = ((2, 1), (1, 1), (3, 1), (2, 0), (1, 0), (3, 0), (0, 1), (0, 0))


def send_label(x, steps, core=0):
    at = lambda z, y, c: (z % NZ) * 4 + (y % NY) * 2 + c % 2
    perm = [
        (at(z, y, c), at(z + steps[c][0], y + steps[c][1], c + core))
        for z in range(NZ)
        for y in range(NY)
        for c in range(2)
    ]
    return lax.ppermute(x, "label", perm)


def swap(x):
    return send_label(x, SOURCE[0], 1)


def to_source(x, p):
    return send_label(x, SOURCE[p])


def from_source(x, p):
    return send_label(x, [(-z, -y) for z, y in SOURCE[p]])


def dp_perm(dx, dy):
    at = lambda x, y: (y % NYH) * 4 + x % NX
    return [(at(x, y), at(x + dx, y + dy)) for y in range(NYH) for x in range(NX)]


VMEM = pl.BlockSpec(memory_space=pltpu.VMEM)
SMEM = pl.BlockSpec(memory_space=pltpu.SMEM)


def call(kernel, name, us, out, specs, args, scratch=(), limit=20):
    return pl.pallas_call(
        kernel,
        out_shape=out,
        in_specs=specs,
        out_specs=jax.tree.map(lambda _: VMEM, out),
        scratch_shapes=list(scratch),
        compiler_params=pltpu.CompilerParams(vmem_limit_bytes=limit * MIB),
        cost_estimate=pl.CostEstimate(
            flops=int(us * 8e8), bytes_accessed=int(us * 1e5), transcendentals=0
        ),
        name=name,
    )(*args)


def array(*shape, dtype=BF16):
    return jax.ShapeDtypeStruct(shape, dtype)


def first_query(me, p, b):
    z, y, c = me // 4, (me // 2) % 2, me % 2
    (z0, y0), (z1, y1) = SOURCE[p]
    z = lax.rem(z + NZ + z0 + c * (z1 - z0), NZ)
    y = lax.rem(y + NY + y0 + c * (y1 - y0), NY)
    return pl.multiple_of((z * 4 + y * 2 + b) * ROWS, ROWS)


def encode_kernel(x_ref, gain_ref, w_in_ref, w_out_ref, out_ref, normed_ref, total_ref):
    i = pl.program_id(0)

    @pl.when(i == 0)
    def _():
        values = x_ref[...].astype(F32)
        meansq = jnp.mean(values * values, axis=-1, keepdims=True)
        normed_ref[...] = (values * lax.rsqrt(meansq + 1e-06) * gain_ref[...]).astype(BF16)
        total_ref[...] = values

    active = jax.nn.gelu(
        jnp.dot(normed_ref[...], w_in_ref[...], preferred_element_type=F32), approximate=True
    ).astype(BF16)
    total_ref[...] += jnp.dot(active, w_out_ref[...], preferred_element_type=F32)

    @pl.when(i == pl.num_programs(0) - 1)
    def _():
        out_ref[...] = total_ref[...].astype(BF16)


def encode(hidden_in, norm_gain, w_in, w_out):
    whole = lambda *shape: pl.BlockSpec(shape, lambda i: (0, 0))
    return pl.pallas_call(
        encode_kernel,
        out_shape=array(ROWS, D),
        grid=(FF // FTILE,),
        in_specs=[
            whole(ROWS, D),
            whole(1, D),
            pl.BlockSpec((D, FTILE), lambda i: (0, i)),
            pl.BlockSpec((FTILE, D), lambda i: (i, 0)),
        ],
        out_specs=whole(ROWS, D),
        scratch_shapes=[pltpu.VMEM((ROWS, D), BF16), pltpu.VMEM((ROWS, D), F32)],
        compiler_params=pltpu.CompilerParams(vmem_limit_bytes=24 * MIB),
        cost_estimate=pl.CostEstimate(
            flops=int(4e9), bytes_accessed=int(1e7), transcendentals=0
        ),
        name="encode",
    )(hidden_in, norm_gain.reshape(1, D), w_in, w_out)


def join_kernel(me_ref, own_ref, other_ref, out_ref):
    c = me_ref[0] % 2
    out_ref[pl.ds(pl.multiple_of(c * ROWS, ROWS), ROWS), :] = own_ref[...]
    out_ref[pl.ds(pl.multiple_of((1 - c) * ROWS, ROWS), ROWS), :] = other_ref[...]


def join(me, own, other):
    return call(
        join_kernel, "join", 0.5, array(PAIR, D), [SMEM, VMEM, VMEM], (me, own, other)
    )


def prepare_kernel(me_ref, sl_ref, pos_ref, bs_ref, *refs):
    half_refs, count_refs = refs[:PAIRS], refs[PAIRS : 2 * PAIRS]
    base_ref, wa_ref, wb_ref = refs[2 * PAIRS :]
    me = me_ref[0]
    slot_rows = lax.broadcasted_iota(jnp.int32, (LBLK, BLOCKS), 0) + me * LBLK
    ids = lax.broadcasted_iota(jnp.int32, (LBLK, BLOCKS), 1).astype(F32)
    here = jnp.sum(jnp.where(bs_ref[...] == slot_rows, ids, 0.0), axis=1, keepdims=True)
    here = jnp.broadcast_to(here, (LBLK, ROWS))
    which = lax.broadcasted_iota(jnp.int32, (K, ROWS), 0)
    shift = lax.broadcasted_iota(jnp.int32, (32, PAIR), 0)
    for p in range(PAIRS):
        for b in range(2):
            lanes = pl.ds(first_query(me, p, b), ROWS)
            sl = sl_ref[:, lanes].astype(F32)
            pos = pos_ref[:, lanes]
            base = jnp.zeros((LBLK, ROWS), F32)
            for k in range(K):
                base = jnp.where(here == sl[k : k + 1], 0.5, base)
            wa = jnp.zeros((LBLK, ROWS), jnp.int32)
            wb = jnp.zeros((LBLK, ROWS), jnp.int32)
            for n in range(P_SIZE):
                kp, jp = pos[n : n + 1] >> 6, pos[n : n + 1] & 63
                bid = jnp.sum(jnp.where(which == kp, sl, 0.0), axis=0, keepdims=True)
                bit = jnp.full((1, ROWS), 1, jnp.int32) << (31 - (jp & 31))
                match = here == bid
                wa = wa | jnp.where(match, jnp.where(jp < 32, bit, 0), 0)
                wb = wb | jnp.where(match, jnp.where(jp < 32, 0, bit), 0)
            out = slice(b * ROWS, (b + 1) * ROWS)
            base_ref[:, out] = base
            wa_ref[:, out] = wa
            wb_ref[:, out] = wb
        count_refs[p][...] = 2.0 * jnp.sum(base_ref[...], axis=0, keepdims=True)
        half_ref = half_refs[p]

        def slot(s, carry):
            base = base_ref[pl.ds(s, 1), :]
            for n, w_ref in enumerate((wa_ref, wb_ref)):
                hit = (w_ref[pl.ds(s, 1), :] << shift) < 0
                rows = pl.ds(pl.multiple_of(s * BL + n * 32, 32), 32)
                half_ref[rows, :] = jnp.where(hit, -base, base).astype(BF16)
            return carry

        lax.fori_loop(0, LBLK, slot, 0, unroll=4)


def prepare(me, sl, pos, bs):
    out = [array(LOCAL, PAIR)] * PAIRS + [array(1, PAIR, dtype=F32)] * PAIRS
    scratch = [pltpu.VMEM((LBLK, PAIR), t) for t in (F32, jnp.int32, jnp.int32)]
    outs = call(
        prepare_kernel, "prepare", 4, out, [SMEM] + [VMEM] * 3, (me, sl, pos, bs), scratch
    )
    return outs[:PAIRS], outs[PAIRS:]


def slope_kernel(q_ref, c_ref, half_ref, count_ref, s_ref, loss_ref, x0_ref, x1_ref):
    x_refs = (x0_ref, x1_ref)
    steps = LOCAL // TILE

    def logits(i):
        x_refs[i % 2][...] = lax.dot_general(
            c_ref[i * TILE : (i + 1) * TILE, :],
            q_ref[...],
            (((1,), (1,)), ((), ())),
            preferred_element_type=F32,
        )

    logits(0)
    losses = [LN2 * BL / 8 * jnp.broadcast_to(count_ref[...], (8, PAIR))[:, t * ROWS : (t + 1) * ROWS]
              for t in range(2)]
    for i in range(steps):
        if i + 1 < steps:
            logits(i + 1)
        for t in range(2):
            lanes = slice(t * ROWS, (t + 1) * ROWS)
            prod = jnp.ones((8, ROWS), F32)
            relu = jnp.zeros((8, ROWS), F32)
            for n in range(TILE // BL):
                rows = slice(i * TILE + n * BL, i * TILE + (n + 1) * BL)
                half = half_ref[rows, lanes].astype(F32)
                y = x_refs[i % 2][n * BL : (n + 1) * BL, lanes] * half
                th = jnp.tanh(y)
                s_ref[rows, lanes] = (half * th + half).astype(BF16)
                u8 = (1.0 + jnp.abs(th)).reshape(BL // 8, 8, ROWS)
                r8 = jnp.maximum(y, 0.0).reshape(BL // 8, 8, ROWS)
                for m in range(BL // 8):
                    prod = prod * u8[m]
                    relu = relu + r8[m]
            losses[t] = losses[t] + (2.0 * relu - jnp.log(prod))
    loss_ref[...] = jnp.sum(jnp.concatenate(losses, axis=1), axis=0, keepdims=True)


def slopes(q, classifier, half, count):
    return call(
        slope_kernel,
        "slopes",
        1.5,
        (array(LOCAL, PAIR), array(1, PAIR, dtype=F32)),
        [VMEM] * 4,
        (q, classifier, half, count),
        [pltpu.VMEM((TILE, PAIR), F32)] * 2,
    )


def loss_rows(row):
    hi = row.astype(BF16)
    rest = row - hi.astype(F32)
    mid = rest.astype(BF16)
    lo = (rest - mid.astype(F32)).astype(BF16)
    return jnp.concatenate([hi, mid, lo, jnp.zeros((EXTRA, D - 3 * ROWS), BF16)], axis=1)


def joined(rows):
    return rows[:, :ROWS] + rows[:, ROWS : 2 * ROWS] + rows[:, 2 * ROWS : 3 * ROWS]


def query_partial(s_ref, c_ref):
    return lax.dot_general(
        s_ref[...], c_ref[...], (((0,), (0,)), ((), ())), preferred_element_type=F32
    )


def loss_block(loss_ref, b):
    return jnp.broadcast_to(loss_ref[:, b * ROWS : (b + 1) * ROWS], (EXTRA, ROWS))


def give_kernel(me_ref, c_ref, s2, s4, s6, s7, l2, l4, l6, l7, g2, g4, g6, keep7, give7, t_ref):
    for s_ref, l_ref, out in ((s2, l2, g2), (s4, l4, g4), (s6, l6, g6)):
        total = query_partial(s_ref, c_ref)
        for b in range(2):
            out[b, :ROWS, :] = total[b * ROWS : (b + 1) * ROWS].astype(BF16)
            out[b, ROWS:, :] = loss_rows(loss_block(l_ref, b))
    total = query_partial(s7, c_ref)
    for b in range(2):
        t_ref[b, :ROWS, :] = total[b * ROWS : (b + 1) * ROWS].astype(BF16)
        t_ref[b, ROWS:, :] = loss_rows(loss_block(l7, b))
    c = me_ref[0] % 2
    keep7[...] = t_ref[c]
    give7[...] = t_ref[1 - c]


def take_kernel(c_ref, s1, s3, s5, l1, l3, l5, r1, r3, r5, keep7, r7, o1, o3, o5, o7):
    for s_ref, l_ref, r_ref, out in ((s1, l1, r1, o1), (s3, l3, r3, o3), (s5, l5, r5, o5)):
        total = query_partial(s_ref, c_ref).astype(BF16).astype(F32)
        for b in range(2):
            out[b, :ROWS, :] = (
                total[b * ROWS : (b + 1) * ROWS] + r_ref[b, :ROWS, :].astype(F32)
            ).astype(BF16)
            out[b, ROWS:, :] = loss_rows(
                loss_block(l_ref, b) + joined(r_ref[b, ROWS:, :].astype(F32))
            )
    total = keep7[...].astype(F32) + r7[...].astype(F32)
    o7[:ROWS, :] = total[:ROWS].astype(BF16)
    o7[ROWS:, :] = loss_rows(joined(total[ROWS:]))


def own_kernel(c_ref, s_ref, l_ref, out_ref):
    total = query_partial(s_ref, c_ref)
    for b in range(2):
        out_ref[b, :ROWS, :] = total[b * ROWS : (b + 1) * ROWS].astype(BF16)
        out_ref[b, ROWS:, :] = loss_rows(loss_block(l_ref, b))


def collect_kernel(me_ref, own, a, b, d, keep, give):
    c = me_ref[0] % 2
    keep[...] = sum(r[c].astype(F32) for r in (own, a, b, d))
    total = sum(r[1 - c].astype(F32) for r in (own, a, b, d))
    give[:ROWS, :] = total[:ROWS].astype(BF16)
    give[ROWS:, :] = loss_rows(joined(total[ROWS:]))


def finish_kernel(keep, other, far, grad_ref, loss_ref):
    total = keep[...] + other[...].astype(F32) + far[...].astype(F32)
    grad_ref[...] = total[:ROWS].astype(BF16)
    loss_ref[...] = joined(total[ROWS : ROWS + 8])[:1]


def class_kernel(count, order_ref, *refs):
    s_refs, q_refs, outs = refs[:PAIRS], refs[PAIRS : 2 * PAIRS], refs[2 * PAIRS :]
    rows = LOCAL // (NX * NYH)
    for n in range(count):
        at = pl.ds(pl.multiple_of(order_ref[n] * rows, rows), rows)
        slope = jnp.concatenate([s[at, :] for s in s_refs], axis=1)
        query = jnp.concatenate([q[...] for q in q_refs], axis=0)
        outs[n][...] = jnp.dot(slope, query, preferred_element_type=F32).astype(BF16)


def class_blocks(order, slope_pairs, pairs):
    count = order.shape[0]
    return call(
        functools.partial(class_kernel, count),
        "class_blocks",
        3.5,
        [array(LOCAL // (NX * NYH), D)] * count,
        [SMEM] + [VMEM] * (2 * PAIRS),
        (order, *slope_pairs, *pairs),
    )


def bound_kernel(me_ref, every_ref, *refs):
    q_refs, out_ref, cent_ref, radii_ref = refs[:PAIRS], refs[PAIRS], refs[-2], refs[-1]
    me = me_ref[0]
    for n in range(BLOCKS // LBLK):
        cent_ref[n * LBLK : (n + 1) * LBLK, :] = every_ref[n, :LBLK, :]
    for n in range(BLOCKS // ROWS):
        terms = sum(every_ref[4 * n + m, LBLK:, :ROWS].astype(F32) for m in range(4))
        radii_ref[:, n * ROWS : (n + 1) * ROWS] = terms[0:1] + terms[1:2] + terms[2:3]
    for p, q in enumerate(q_refs):
        for b in range(2):
            rows = slice(b * ROWS, (b + 1) * ROWS)
            value = q[rows, :].astype(F32)
            norm = jnp.sqrt(jnp.sum(value * value, axis=1, keepdims=True))
            score = lax.dot_general(
                q[rows, :], cent_ref[...], (((1,), (1,)), ((), ())), preferred_element_type=F32
            )
            top = jnp.max(score + norm * radii_ref[...], axis=1, keepdims=True)
            out_ref[:, pl.ds(first_query(me, p, b), ROWS)] = jnp.broadcast_to(
                top, (ROWS, ROWS)
            ).T[:1]


def after(value, *others):
    return lax.optimization_barrier((value, others))[0]


def on_device(
    hidden_in,
    norm_gain,
    w_in,
    w_out,
    classifier,
    centroids,
    radii,
    shortlist,
    positives,
    block_slot,
):
    label = lax.axis_index("label")
    dp = lax.axis_index("dp")
    me = label.astype(jnp.int32).reshape(1)

    hi = lax.reduce_precision(radii, 8, 7)
    mid = lax.reduce_precision(radii - hi, 8, 7)
    lo = lax.reduce_precision(radii - hi - mid, 8, 7)
    terms = jnp.tile(jnp.stack([hi, mid, lo]).astype(BF16), (1, D // LBLK))
    terms = jnp.where(jnp.arange(D) // LBLK == label % 4, terms, 0)
    packed = jnp.concatenate([centroids, jnp.pad(terms, ((0, CROWS - LBLK - 3), (0, 0)))], axis=0)
    every = lax.all_gather(packed, "label", axis=0)

    encoded = encode(hidden_in, norm_gain, w_in, w_out)

    pairs = [None] * PAIRS
    far = from_source(encoded, 7)
    pairs[0] = join(me, encoded, swap(encoded))
    for p in (1, 3, 5):
        pairs[p] = from_source(pairs[0], p)
        pairs[p + 1] = swap(pairs[p])
    pairs[7] = join(me, far, swap(far))

    halves, counts = prepare(
        after(me, encoded), shortlist.T, positives.T, block_slot.reshape(1, -1)
    )
    slope_pairs, losses = [None] * PAIRS, [None] * PAIRS
    for p in range(PAIRS):
        slope_pairs[p], losses[p] = slopes(pairs[p], classifier, halves[p], counts[p])

    order = jnp.stack(
        [((dp // NX + dy) % NYH) * NX + (dp % NX + dx) % NX for dx, dy in DP_ORDER]
    ).astype(jnp.int32)
    blocks = class_blocks(order[:4], slope_pairs, pairs)
    blocks = blocks + class_blocks(after(order[4:], blocks[0]), slope_pairs, pairs)
    class_total = blocks[-1].astype(F32)
    for (dx, dy), block in zip(DP_ORDER[:-1], blocks):
        class_total = class_total + lax.ppermute(block, "dp", dp_perm(dx, dy)).astype(F32)

    part = array(2, ROWS + EXTRA, D)
    half_part = array(ROWS + EXTRA, D)
    s, l = slope_pairs, losses
    g2, g4, g6, keep7, give7 = call(
        give_kernel,
        "give",
        4.5,
        (part, part, part, half_part, half_part),
        [SMEM] + [VMEM] * 9,
        (after(me, blocks[-1]), classifier, s[2], s[4], s[6], s[7], l[2], l[4], l[6], l[7]),
        [pltpu.VMEM((2, ROWS + EXTRA, D), BF16)],
    )
    r1, r3, r5, r7 = swap(g2), swap(g4), swap(g6), swap(give7)
    bound_top = call(
        bound_kernel,
        "bounds",
        4,
        array(1, PAIRS * PAIR, dtype=F32),
        [SMEM] + [VMEM] * (PAIRS + 1),
        (after(me, give7), every, *pairs),
        [pltpu.VMEM((BLOCKS, D), BF16), pltpu.VMEM((1, BLOCKS), F32)],
    )
    o1, o3, o5, o7 = call(
        take_kernel,
        "take",
        4,
        (part, part, part, half_part),
        [VMEM] * 12,
        (classifier, s[1], s[3], s[5], l[1], l[3], l[5], r1, r3, r5, keep7, r7),
    )
    own = call(own_kernel, "own", 1.2, part, [VMEM] * 3, (classifier, s[0], l[0]))
    keep, give = call(
        collect_kernel,
        "collect",
        1,
        (array(ROWS + EXTRA, D, dtype=F32), half_part),
        [SMEM] + [VMEM] * 4,
        (me, own, to_source(o1, 1), to_source(o3, 3), to_source(o5, 5)),
    )
    query_grad, loss = call(
        finish_kernel,
        "finish",
        1,
        (array(ROWS, D), array(1, ROWS, dtype=F32)),
        [VMEM] * 3,
        (keep, swap(give), to_source(o7, 7)),
    )
    return (
        bound_top.reshape(-1),
        loss.reshape(-1),
        query_grad,
        class_total.astype(BF16),
    )


def solution(mesh):
    placed = (
        P(("dp", "label"), None),
        P(),
        P(),
        P(),
        P("label", None),
        P("label", None),
        P("label"),
        P("dp", None),
        P("dp", None),
        P(),
    )
    return jax.shard_map(
        on_device,
        mesh=mesh,
        in_specs=placed,
        out_specs=(P("dp"), P(("dp", "label")), P(("dp", "label"), None), P(("label", "dp"), None)),
        check_vma=False,
    )
```

```python
import functools

import jax
import jax.numpy as jnp
from jax import lax
from jax.experimental import pallas as pl
from jax.experimental.pallas import tpu as pltpu
from jax.sharding import PartitionSpec as P

F32 = jnp.float32
BF16 = jnp.bfloat16

NZ, NY = 4, 2
NX, NYH = 4, 2
ROWS = 128
PAIR = 2 * ROWS
PAIRS = 8
EXTRA = 16
D = 768
FF = 3072
FTILE = 512
BL = 64
K = 16
P_SIZE = 4
LBLK = 32
LOCAL = LBLK * BL
BLOCKS = 512
CROWS = 48
TILE = 256
TILES = LOCAL // TILE
HALF = LOCAL // 2
SLOTS = TILE // BL
PIECE_SLOTS = 2
CWIDTH = D + 128
LN2 = 0.6931471805599453
MIB = 1024 * 1024

SOURCE = (
    ((0, 0), (0, 0)),
    ((-1, 0), (1, 0)),
    ((1, 0), (-1, 0)),
    ((0, 1), (2, 0)),
    ((2, 0), (0, 1)),
    ((-1, 1), (1, 1)),
    ((1, 1), (-1, 1)),
    ((2, 1), (2, 1)),
)

DP_STEPS = (2, 1, 3, 0)
PIECE = 128


def send_label(x, steps, core=0):
    at = lambda z, y, c: (z % NZ) * 4 + (y % NY) * 2 + c % 2
    perm = [
        (at(z, y, c), at(z + steps[c][0], y + steps[c][1], c + core))
        for z in range(NZ)
        for y in range(NY)
        for c in range(2)
    ]
    return lax.ppermute(x, "label", perm)


def swap(x):
    return send_label(x, SOURCE[0], 1)


def to_source(x, p):
    return send_label(x, SOURCE[p])


def from_source(x, p):
    return send_label(x, [(-z, -y) for z, y in SOURCE[p]])


def dp_perm(dx, dy):
    at = lambda x, y: (y % NYH) * 4 + x % NX
    return [(at(x, y), at(x + dx, y + dy)) for y in range(NYH) for x in range(NX)]


VMEM = pl.BlockSpec(memory_space=pltpu.VMEM)
SMEM = pl.BlockSpec(memory_space=pltpu.SMEM)
ANY = pl.BlockSpec(memory_space=pl.ANY)
HBM = pl.BlockSpec(memory_space=pltpu.HBM)


def call(kernel, name, us, out, specs, args, scratch=(), limit=60, out_specs=None):
    return pl.pallas_call(
        kernel,
        out_shape=out,
        in_specs=specs,
        out_specs=out_specs or jax.tree.map(lambda _: VMEM, out),
        scratch_shapes=list(scratch),
        compiler_params=pltpu.CompilerParams(vmem_limit_bytes=limit * MIB),
        cost_estimate=pl.CostEstimate(
            flops=int(us * 8e8), bytes_accessed=int(us * 1e5), transcendentals=0
        ),
        name=name,
    )(*args)


def array(*shape, dtype=BF16):
    return jax.ShapeDtypeStruct(shape, dtype)


def first_query(me, p, b):
    z, y, c = me // 4, (me // 2) % 2, me % 2
    (z0, y0), (z1, y1) = SOURCE[p]
    z = lax.rem(z + NZ + z0 + c * (z1 - z0), NZ)
    y = lax.rem(y + NY + y0 + c * (y1 - y0), NY)
    core = lax.rem(c + b + (p in (2, 4, 6)), 2)
    return pl.multiple_of((z * 4 + y * 2 + core) * ROWS, ROWS)


def piece_at(dp, n):
    half, dx, dy = n // 8, DP_STEPS[n % 8 // 2], n % 2
    return (lax.rem(dp // NX + dy, NYH) * NX + lax.rem(dp % NX + dx, NX)) * 2 + half


def encode_kernel(x_ref, gain_ref, w_in_hbm, w_out_hbm, out_ref, w_in_ref, w_out_ref, sems):
    parts = [slice(i * FTILE, (i + 1) * FTILE) for i in range(FF // FTILE)]
    copies = []
    for i, part in enumerate(parts):
        into = pltpu.make_async_copy(w_in_hbm.at[:, part], w_in_ref.at[:, part], sems.at[0, i])
        out = pltpu.make_async_copy(w_out_hbm.at[part, :], w_out_ref.at[part, :], sems.at[1, i])
        into.start()
        out.start()
        copies.append((into, out))
    values = x_ref[...].astype(F32)
    meansq = jnp.mean(values * values, axis=-1, keepdims=True)
    normed = (values * lax.rsqrt(meansq + 1e-06) * gain_ref[...].reshape(1, D)).astype(BF16)
    total = values
    for part, (into, out) in zip(parts, copies):
        into.wait()
        active = jax.nn.gelu(
            jnp.dot(normed, w_in_ref[:, part], preferred_element_type=F32), approximate=True
        ).astype(BF16)
        out.wait()
        total = total + jnp.dot(active, w_out_ref[part, :], preferred_element_type=F32)
    out_ref[...] = total.astype(BF16)


def encode(hidden_in, norm_gain, w_in, w_out):
    return pl.pallas_call(
        encode_kernel,
        out_shape=array(ROWS, D),
        in_specs=[VMEM, VMEM, HBM, HBM],
        out_specs=VMEM,
        scratch_shapes=[
            pltpu.VMEM((D, FF), BF16),
            pltpu.VMEM((FF, D), BF16),
            pltpu.SemaphoreType.DMA((2, FF // FTILE)),
        ],
        compiler_params=pltpu.CompilerParams(vmem_limit_bytes=60 * MIB),
        cost_estimate=pl.CostEstimate(
            flops=int(4e9), bytes_accessed=int(1e7), transcendentals=0
        ),
        name="encode",
    )(hidden_in, norm_gain, w_in, w_out)


def prepare(me, dp, sl_ref, pos_ref, bs_ref, base_ref, wa_ref, wb_ref):
    slot_rows = lax.broadcasted_iota(jnp.int32, (LBLK, BLOCKS), 0)
    place, piece = slot_rows // PIECE_SLOTS, jnp.zeros_like(slot_rows)
    for n in range(LOCAL // PIECE):
        piece = jnp.where(place == n, piece_at(dp, n), piece)
    slot_rows = slot_rows % PIECE_SLOTS + piece * PIECE_SLOTS + me * LBLK
    ids = lax.broadcasted_iota(jnp.int32, (LBLK, BLOCKS), 1).astype(F32)
    here = jnp.sum(jnp.where(bs_ref[...] == slot_rows, ids, 0.0), axis=1, keepdims=True)
    here = jnp.broadcast_to(here, (LBLK, ROWS))
    which = lax.broadcasted_iota(jnp.int32, (K, ROWS), 0)
    for p in range(PAIRS):
        for b in range(2):
            lanes = pl.ds(first_query(me, p, b), ROWS)
            sl = sl_ref[:, lanes].astype(F32)
            pos = pos_ref[:, lanes]
            base = jnp.zeros((LBLK, ROWS), F32)
            for k in range(K):
                base = jnp.where(here == sl[k : k + 1], 0.5, base)
            wa = jnp.zeros((LBLK, ROWS), jnp.int32)
            wb = jnp.zeros((LBLK, ROWS), jnp.int32)
            for n in range(P_SIZE):
                kp, jp = pos[n : n + 1] >> 6, pos[n : n + 1] & 63
                bid = jnp.sum(jnp.where(which == kp, sl, 0.0), axis=0, keepdims=True)
                bit = jnp.full((1, ROWS), 1, jnp.int32) << (31 - (jp & 31))
                match = here == bid
                wa = wa | jnp.where(match, jnp.where(jp < 32, bit, 0), 0)
                wb = wb | jnp.where(match, jnp.where(jp < 32, 0, bit), 0)
            out = slice(b * ROWS, (b + 1) * ROWS)
            base_ref[p, :, out] = base
            wa_ref[p, :, out] = wa
            wb_ref[p, :, out] = wb


def loss_rows(row):
    hi = row.astype(BF16)
    rest = row - hi.astype(F32)
    mid = rest.astype(BF16)
    lo = (rest - mid.astype(F32)).astype(BF16)
    return jnp.concatenate([hi, mid, lo, jnp.zeros((EXTRA, D - 3 * ROWS), BF16)], axis=1)


def joined(rows):
    return rows[:, :ROWS] + rows[:, ROWS : 2 * ROWS] + rows[:, 2 * ROWS : 3 * ROWS]


def add_pair(a_ref, b_ref, out_ref):
    for b in [()] if len(out_ref.shape) == 2 else [(0,), (1,)]:
        grad, loss = b + (slice(0, ROWS),), b + (slice(ROWS, ROWS + EXTRA),)
        out_ref[grad] = (a_ref[grad].astype(F32) + b_ref[grad].astype(F32)).astype(BF16)
        out_ref[loss] = loss_rows(joined(a_ref[loss].astype(F32) + b_ref[loss].astype(F32)))


def slopes(numbers, at, tiles, q_ref, c_ref, flags, s_ref, x_refs, wait, done):
    base_ref, wa_ref, wb_ref = flags
    steps = [(j, i) for j in range(len(numbers)) for i in tiles]
    shift = lax.broadcasted_iota(jnp.int32, (32, ROWS), 0)

    def logits(n):
        j, i = steps[n]
        wait(j, i)
        j += at
        i -= c_ref.shape[0] < LOCAL and tiles[0]
        x_refs[n % 2][...] = lax.dot_general(
            c_ref[i * TILE : (i + 1) * TILE, :],
            q_ref[j * PAIR : (j + 1) * PAIR, :],
            (((1,), (1,)), ((), ())),
            preferred_element_type=F32,
        )

    logits(0)
    for k, (j, i) in enumerate(steps):
        p = numbers[j]
        if k + 1 < len(steps):
            logits(k + 1)
        if i == tiles[0]:
            slot = slice(tiles[0] * SLOTS, (tiles[-1] + 1) * SLOTS)
            count = 2.0 * jnp.sum(base_ref[p, slot, :], axis=0, keepdims=True)
            losses = [
                jnp.broadcast_to((LN2 * BL / 8) * count[:, t * ROWS : (t + 1) * ROWS], (8, ROWS))
                for t in range(2)
            ]
        for t in range(2):
            lanes = slice(t * ROWS, (t + 1) * ROWS)
            into = slice((at + j) * PAIR + t * ROWS, (at + j) * PAIR + (t + 1) * ROWS)
            prod = jnp.ones((8, ROWS), F32)
            relu = jnp.zeros((8, ROWS), F32)
            for n in range(TILE // BL):
                slot = slice(i * (TILE // BL) + n, i * (TILE // BL) + n + 1)
                rows = slice(i * TILE + n * BL, i * TILE + (n + 1) * BL)
                base = base_ref[p, slot, lanes]
                bits = jnp.concatenate(
                    [wa_ref[p, slot, lanes] << shift, wb_ref[p, slot, lanes] << shift], axis=0
                )
                half = jnp.where(bits < 0, -base, base)
                y = x_refs[k % 2][n * BL : (n + 1) * BL, lanes] * half
                th = jnp.tanh(y)
                s_ref[rows, into] = (half * th + half).astype(BF16)
                u8 = (1.0 + jnp.abs(th)).reshape(BL // 8, 8, ROWS)
                r8 = jnp.maximum(y, 0.0).reshape(BL // 8, 8, ROWS)
                for m in range(BL // 8):
                    prod = prod * u8[m]
                    relu = relu + r8[m]
            losses[t] = losses[t] + (2.0 * relu - jnp.log(prod))
        if i == tiles[-1]:
            done(j, jnp.sum(jnp.concatenate(losses, axis=1), axis=0, keepdims=True))


PART = array(2, ROWS + EXTRA, D)
HALF_PART = array(ROWS + EXTRA, D)
NEAR, REST = (0, 7), (1, 2, 3, 4, 5, 6)
FAR_Q = len(NEAR) * PAIR
FLAGS = tuple(array(PAIRS, LBLK, PAIR, dtype=t) for t in (F32, jnp.int32, jnp.int32))
X_SCRATCH = [pltpu.VMEM((TILE, PAIR), F32)] * 2
CLASS_ROWS = LOCAL // (NX * NYH)


def query_part(s_ref, j, c_ref, loss, outs):
    total = lax.dot_general(
        s_ref[:, j * PAIR : (j + 1) * PAIR],
        c_ref[...],
        (((0,), (0,)), ((), ())),
        preferred_element_type=F32,
    )
    for b, out in enumerate(outs):
        out[:ROWS, :] = total[b * ROWS : (b + 1) * ROWS].astype(BF16)
        row = jnp.broadcast_to(loss[:, b * ROWS : (b + 1) * ROWS], (EXTRA, ROWS))
        out[ROWS:, :] = loss_rows(row)


class Copies:
    def __init__(self, sems):
        self.sems, self.count = sems, 0

    def start(self, source, target):
        copy = pltpu.make_async_copy(source, target, self.sems.at[self.count])
        copy.start()
        self.count += 1
        return copy


def fill(copies, sources, q_ref, row):
    started = []
    for source in sources:
        rows = source.shape[0]
        started.append(copies.start(source, q_ref.at[row : row + rows, :]))
        row += rows
    return started


def label_copies(copies, dp_ref, c_hbm, c_ref, tiles):
    started = []
    for n, i in enumerate(tiles):
        both = []
        for b in range(2):
            at = piece_at(dp_ref[0], 2 * i + b)
            rows = pl.ds(pl.multiple_of(at * PIECE, PIECE), PIECE)
            into = slice(n * TILE + b * PIECE, n * TILE + (b + 1) * PIECE)
            both.append(copies.start(c_hbm.at[rows, :], c_ref.at[into, :]))
        started.append(both)
    return started


def wait_all(copies):
    for copy in copies:
        copy.wait()


def near_kernel(me_ref, dp_ref, sl_ref, pos_ref, bs_ref, c_hbm, own, other, far, far2,
                s_hbm, part0, keep7, give7, base_ref, wa_ref, wb_ref,
                c_ref, q_ref, s_ref, x0_ref, x1_ref, sems):
    copies = Copies(sems)
    queries = fill(copies, (own, other), q_ref, 0)
    labels = label_copies(copies, dp_ref, c_hbm, c_ref, range(TILES))
    queries += fill(copies, (far, far2), q_ref, PAIR)
    prepare(me_ref[0], dp_ref[0], sl_ref, pos_ref, bs_ref, base_ref, wa_ref, wb_ref)
    outs = ((part0.at[0], part0.at[1]), (keep7, give7))
    stored = []

    def wait(j, i):
        if i == 0:
            queries[2 * j].wait()
            queries[2 * j + 1].wait()
        if j == 0:
            wait_all(labels[i])

    def done(j, loss):
        columns = slice(j * PAIR, (j + 1) * PAIR)
        stored.append(copies.start(s_ref.at[:, columns], s_hbm.at[:, columns]))
        query_part(s_ref, j, c_ref, loss, outs[j])

    slopes(NEAR, 0, range(TILES), q_ref, c_ref, (base_ref, wa_ref, wb_ref), s_ref, (x0_ref, x1_ref), wait, done)
    for copy in stored:
        copy.wait()


def gate_kernel(dep_ref, *refs):
    del dep_ref, refs


def gate(dep, *arrays):
    return pl.pallas_call(
        gate_kernel,
        out_shape=tuple(array(*a.shape) for a in arrays),
        in_specs=[ANY] * (1 + len(arrays)),
        out_specs=(ANY,) * len(arrays),
        input_output_aliases={n + 1: n for n in range(len(arrays))},
        cost_estimate=pl.CostEstimate(flops=1000, bytes_accessed=1000, transcendentals=0),
        name="gate",
    )(dep, *arrays)


REST_Q = len(REST) * PAIR


def class_part(s_ref, row, q_ref, blocks):
    for n in range(0, len(blocks), 2):
        at = row + n * TILE
        total = jnp.dot(s_ref[at : at + 2 * TILE, :], q_ref[...], preferred_element_type=F32)
        blocks[n][...] = total[:TILE].astype(BF16)
        blocks[n + 1][...] = total[TILE:].astype(BF16)


def first_kernel(dp_ref, base_hbm, wa_hbm, wb_hbm, c_hbm, s_near, *refs):
    n = len(PIECES)
    pieces, (s_hbm, loss_ref), blocks = refs[:n], refs[n : n + 2], refs[n + 2 : n + 6]
    base_ref, wa_ref, wb_ref, c_ref, q_ref, s_ref, x0_ref, x1_ref, sems = refs[n + 6 :]
    copies = Copies(sems)
    flags = [
        copies.start(source, target)
        for source, target in ((base_hbm, base_ref), (wa_hbm, wa_ref), (wb_hbm, wb_ref))
    ]
    queries = fill(copies, pieces[4:5], q_ref, FAR_Q)
    labels = label_copies(copies, dp_ref, c_hbm, c_ref, range(TILES // 2))
    queries += fill(copies, pieces[5:], q_ref, FAR_Q + PAIR)
    early = fill(copies, pieces[:4], q_ref, 0)
    early.append(copies.start(s_near.at[:HALF, :], s_ref.at[:, :FAR_Q]))
    stored = []
    for copy in flags:
        copy.wait()

    def wait(j, i):
        if i == 0:
            queries[j].wait()
        if j == 0:
            wait_all(labels[i])

    def done(j, loss):
        at = slice(FAR_Q + j * PAIR, FAR_Q + (j + 1) * PAIR)
        columns = slice(j * PAIR, (j + 1) * PAIR)
        stored.append(copies.start(s_ref.at[:, at], s_hbm.at[:, columns]))
        loss_ref[:, columns] = loss

    slopes(REST, len(NEAR), range(TILES // 2), q_ref, c_ref, (base_ref, wa_ref, wb_ref), s_ref,
           (x0_ref, x1_ref), wait, done)
    for copy in early:
        copy.wait()
    class_part(s_ref, 0, q_ref, blocks)
    for copy in stored:
        copy.wait()


def second_kernel(dp_ref, loss_ref, base_hbm, wa_hbm, wb_hbm, c_hbm, s_near, s_first, *refs):
    n, m = len(PIECES), len(PIECES) + len(REST)
    pieces, parts, blocks = refs[:n], refs[n:m], refs[m : m + 4]
    base_ref, wa_ref, wb_ref, c_ref, q_ref, s_ref, x0_ref, x1_ref, sems = refs[m + 4 :]
    copies = Copies(sems)
    flags = [
        copies.start(source, target)
        for source, target in ((base_hbm, base_ref), (wa_hbm, wa_ref), (wb_hbm, wb_ref))
    ]
    queries = fill(copies, pieces[4:5], q_ref, FAR_Q)
    half = range(TILES // 2, TILES)
    labels = label_copies(copies, dp_ref, c_hbm, c_ref.at[HALF:, :], half)
    queries += fill(copies, pieces[5:], q_ref, FAR_Q + PAIR)
    before = [copies.start(s_first, s_ref.at[:HALF, FAR_Q:])]
    before += sum(label_copies(copies, dp_ref, c_hbm, c_ref, range(TILES // 2)), [])
    early = fill(copies, pieces[:4], q_ref, 0)
    early.append(copies.start(s_near.at[HALF:, :], s_ref.at[HALF:, :FAR_Q]))
    for copy in flags:
        copy.wait()

    def wait(j, i):
        if i == half[0]:
            queries[j].wait()
        if j == 0:
            wait_all(labels[i - half[0]])

    def done(j, loss):
        if j == 0:
            for copy in before:
                copy.wait()
        loss = loss + loss_ref[:, j * PAIR : (j + 1) * PAIR]
        query_part(s_ref, len(NEAR) + j, c_ref, loss, (parts[j].at[0], parts[j].at[1]))

    slopes(REST, len(NEAR), half, q_ref, c_ref, (base_ref, wa_ref, wb_ref), s_ref,
           (x0_ref, x1_ref), wait, done)
    for copy in early:
        copy.wait()
    class_part(s_ref, HALF, q_ref, blocks)


def sum_kernel(count, *refs):
    for n in range(count):
        add_pair(refs[2 * n], refs[2 * n + 1], refs[len(refs) - count + n])


def along_x_kernel(own, a, b, c, dep_ref, keep, give):
    del dep_ref
    total = sum(r[...].astype(F32) for r in (own, a, b, c))
    keep[...] = total[:PIECE]
    give[...] = total[PIECE:].astype(BF16)


def along_x(blocks, dep):
    *sent, own = blocks
    moved = [
        lax.ppermute(block, "dp", dp_perm(dx, 0)) for dx, block in zip(DP_STEPS, sent)
    ]
    return call(
        along_x_kernel,
        "along_x",
        1,
        (array(PIECE, D, dtype=F32), array(PIECE, D)),
        [VMEM] * 4 + [ANY],
        (own, *moved, dep),
    )


def along_y_kernel(keep0, r0, keep1, r1, out):
    for half, (keep, r) in enumerate(((keep0, r0), (keep1, r1))):
        out[half * PIECE : (half + 1) * PIECE, :] = (keep[...] + r[...].astype(F32)).astype(BF16)


def collect_kernel(own, a, b, d, keep, give):
    keep[...] = sum(r[0].astype(F32) for r in (own, a, b, d))
    total = sum(r[1].astype(F32) for r in (own, a, b, d))
    give[:ROWS, :] = total[:ROWS].astype(BF16)
    give[ROWS:, :] = loss_rows(joined(total[ROWS:]))


def finish_kernel(keep, other, far, grad_ref, loss_ref):
    total = keep[...] + other[...].astype(F32) + far[...].astype(F32)
    grad_ref[...] = total[:ROWS].astype(BF16)
    loss_ref[...] = joined(total[ROWS : ROWS + 8])[:1]


PIECES = ((0, 0), (0, 1), (7, 0), (7, 1)) + tuple((p, 0) for p in REST)


def bound_kernel(me_ref, every_ref, *refs):
    q_refs, (_, out_ref, cent_ref, radii_ref) = refs[: len(PIECES)], refs[len(PIECES) :]
    me = me_ref[0]
    for n in range(BLOCKS // LBLK):
        rows = slice(n * LBLK, (n + 1) * LBLK)
        cent_ref[rows, :] = every_ref[n, :LBLK, :D]
        terms = every_ref[n, :LBLK, D:].astype(F32)
        radius = terms[:, 0:1] + terms[:, 1:2] + terms[:, 2:3]
        radii_ref[rows, :] = jnp.broadcast_to(radius, (LBLK, ROWS))
    ones = jnp.ones((8, D), BF16)
    over_row = lambda a, b: lax.dot_general(
        a, b, (((1,), (1,)), ((), ())), preferred_element_type=F32
    )
    for (p, half), q in zip(PIECES, q_refs):
        value = q[...].astype(F32)
        square = value * value
        high = square.astype(BF16)
        low = (square - high.astype(F32)).astype(BF16)
        norm = jnp.sqrt(over_row(ones, high) + over_row(ones, low))[:1]
        score = over_row(cent_ref[...], q[...])
        for b in range(q.shape[0] // ROWS):
            lanes = slice(b * ROWS, (b + 1) * ROWS)
            bound = score[:, lanes] + radii_ref[...] * norm[:, lanes]
            out_ref[:, pl.ds(first_query(me, p, half + b), ROWS)] = jnp.max(
                bound, axis=0, keepdims=True
            )


def after(value, *others):
    return lax.optimization_barrier((value, others))[0]


def on_device(
    hidden_in,
    norm_gain,
    w_in,
    w_out,
    classifier,
    centroids,
    radii,
    shortlist,
    positives,
    block_slot,
):
    label = lax.axis_index("label")
    dp = lax.axis_index("dp")
    me = label.astype(jnp.int32).reshape(1)

    hi = lax.reduce_precision(radii, 8, 7)
    mid = lax.reduce_precision(radii - hi, 8, 7)
    lo = lax.reduce_precision(radii - hi - mid, 8, 7)
    terms = jnp.stack([hi, mid, lo], axis=1).astype(BF16)
    packed = jnp.concatenate([centroids, jnp.pad(terms, ((0, 0), (0, CWIDTH - D - 3)))], axis=1)
    every = lax.all_gather(jnp.pad(packed, ((0, CROWS - LBLK), (0, 0))), "label", axis=0)

    encoded = encode(hidden_in, norm_gain, w_in, w_out)

    far = from_source(encoded, 7)
    other = swap(encoded)
    pair = jnp.concatenate([encoded, other])
    near = (encoded, other, far, swap(far))
    dp = dp.astype(jnp.int32).reshape(1)
    s_near, part0, keep7, give7, *flags = call(
        near_kernel,
        "near",
        6,
        (array(LOCAL, FAR_Q), PART, HALF_PART, HALF_PART) + FLAGS,
        [SMEM] * 2 + [VMEM] * 3 + [ANY] * 5,
        (me, dp, shortlist.T, positives.T, block_slot.reshape(1, -1), classifier, *near),
        [
            pltpu.VMEM((LOCAL, D), BF16),
            pltpu.VMEM((FAR_Q, D), BF16),
            pltpu.VMEM((LOCAL, FAR_Q), BF16),
            *X_SCRATCH,
            pltpu.SemaphoreType.DMA((4 + 2 * TILES + 2,)),
        ],
        out_specs=(ANY,) + (VMEM,) * 6,
    )
    received = gate(keep7, *(from_source(pair, p) for p in (1, 3, 5)))
    rest = tuple(r for q in received for r in (q, swap(q)))
    pieces = near + rest
    flag_scratch = [pltpu.VMEM(f.shape, f.dtype) for f in FLAGS]
    s_first, loss_first, *first = call(
        first_kernel,
        "first_half",
        12,
        (array(HALF, REST_Q), array(1, REST_Q, dtype=F32)) + (array(TILE, D),) * 4,
        [SMEM] + [ANY] * (5 + len(pieces)),
        (dp, *flags, classifier, s_near, *pieces),
        flag_scratch
        + [
            pltpu.VMEM((HALF, D), BF16),
            pltpu.VMEM((PAIRS * PAIR, D), BF16),
            pltpu.VMEM((HALF, PAIRS * PAIR), BF16),
            *X_SCRATCH,
            pltpu.SemaphoreType.DMA((3 + len(pieces) + TILES + 1 + len(REST),)),
        ],
        out_specs=(ANY,) + (VMEM,) * 5,
    )
    *parts, = call(
        second_kernel,
        "second_half",
        18,
        (PART,) * len(REST) + (array(TILE, D),) * 4,
        [SMEM, VMEM] + [ANY] * (6 + len(pieces)),
        (dp, loss_first, *flags, classifier, s_near, s_first, *pieces),
        flag_scratch
        + [
            pltpu.VMEM((LOCAL, D), BF16),
            pltpu.VMEM((PAIRS * PAIR, D), BF16),
            pltpu.VMEM((LOCAL, PAIRS * PAIR), BF16),
            *X_SCRATCH,
            pltpu.SemaphoreType.DMA((3 + len(pieces) + 2 * TILES + 2,)),
        ],
    )
    keep_first, give_first = along_x(first, loss_first)

    sum1, sum3, sum5, sum7 = call(
        functools.partial(sum_kernel, 4),
        "sums",
        2,
        (PART, PART, PART, HALF_PART),
        [VMEM] * 8 + [ANY],
        (
            *(t for n in (0, 2, 4) for t in (parts[n], swap(parts[n + 1]))),
            keep7,
            swap(give7),
            give_first,
        ),
    )
    bound_top = call(
        bound_kernel,
        "bounds",
        6,
        array(1, PAIRS * PAIR, dtype=F32),
        [SMEM] + [VMEM] * (len(PIECES) + 1) + [ANY],
        (me, every, *pieces, sum7),
        [pltpu.VMEM((BLOCKS, D), BF16), pltpu.VMEM((BLOCKS, ROWS), F32)],
    )
    far_part = to_source(sum7, 7)
    keep, give = call(
        collect_kernel,
        "collect",
        1,
        (array(ROWS + EXTRA, D, dtype=F32), HALF_PART),
        [VMEM] * 4,
        (part0, to_source(sum1, 1), to_source(sum3, 3), to_source(sum5, 5)),
    )
    query_grad, loss = call(
        finish_kernel,
        "finish",
        1,
        (array(ROWS, D), array(1, ROWS, dtype=F32)),
        [VMEM] * 3,
        (keep, swap(give), far_part),
    )
    keep_second, give_second = along_x(parts[len(REST) :], bound_top)
    class_grad = call(
        along_y_kernel,
        "along_y",
        1,
        array(2 * PIECE, D),
        [VMEM] * 4,
        (
            keep_first,
            lax.ppermute(give_first, "dp", dp_perm(0, 1)),
            keep_second,
            lax.ppermute(give_second, "dp", dp_perm(0, 1)),
        ),
    )
    return bound_top.reshape(-1), loss.reshape(-1), query_grad, class_grad


def solution(mesh):
    placed = (
        P(("dp", "label"), None),
        P(),
        P(),
        P(),
        P("label", None),
        P("label", None),
        P("label"),
        P("dp", None),
        P("dp", None),
        P(),
    )
    return jax.shard_map(
        on_device,
        mesh=mesh,
        in_specs=placed,
        out_specs=(P("dp"), P(("dp", "label")), P(("dp", "label"), None), P(("label", "dp"), None)),
        check_vma=False,
    )
```

```python
import functools

import jax
import jax.numpy as jnp
from jax import lax
from jax.experimental import pallas as pl
from jax.experimental.pallas import tpu as pltpu
from jax.sharding import PartitionSpec as P

F32 = jnp.float32
BF16 = jnp.bfloat16

NZ, NY = 4, 2
NX, NYH = 4, 2
ROWS = 128
PAIR = 2 * ROWS
PAIRS = 8
EXTRA = 16
D = 768
FF = 3072
FTILE = 512
BL = 64
K = 16
P_SIZE = 4
LBLK = 32
LOCAL = LBLK * BL
BLOCKS = 512
CROWS = 48
TILE = 256
TILES = LOCAL // TILE
HALF = LOCAL // 2
SLOTS = TILE // BL
PIECE_SLOTS = 2
CWIDTH = D + 128
LN2 = 0.6931471805599453
MIB = 1024 * 1024

SOURCE = (
    ((0, 0), (0, 0)),
    ((-1, 0), (1, 0)),
    ((1, 0), (-1, 0)),
    ((0, 1), (2, 0)),
    ((2, 0), (0, 1)),
    ((-1, 1), (1, 1)),
    ((1, 1), (-1, 1)),
    ((2, 1), (2, 1)),
)

DP_STEPS = (2, 1, 3, 0)
PIECE = 128


def send_label(x, steps, core=0):
    at = lambda z, y, c: (z % NZ) * 4 + (y % NY) * 2 + c % 2
    perm = [
        (at(z, y, c), at(z + steps[c][0], y + steps[c][1], c + core))
        for z in range(NZ)
        for y in range(NY)
        for c in range(2)
    ]
    return lax.ppermute(x, "label", perm)


def swap(x):
    return send_label(x, SOURCE[0], 1)


def to_source(x, p):
    return send_label(x, SOURCE[p])


def from_source(x, p):
    return send_label(x, [(-z, -y) for z, y in SOURCE[p]])


def dp_perm(dx, dy):
    at = lambda x, y: (y % NYH) * 4 + x % NX
    return [(at(x, y), at(x + dx, y + dy)) for y in range(NYH) for x in range(NX)]


VMEM = pl.BlockSpec(memory_space=pltpu.VMEM)
SMEM = pl.BlockSpec(memory_space=pltpu.SMEM)
ANY = pl.BlockSpec(memory_space=pl.ANY)
HBM = pl.BlockSpec(memory_space=pltpu.HBM)


def call(kernel, name, us, out, specs, args, scratch=(), limit=60, out_specs=None):
    return pl.pallas_call(
        kernel,
        out_shape=out,
        in_specs=specs,
        out_specs=out_specs or jax.tree.map(lambda _: VMEM, out),
        scratch_shapes=list(scratch),
        compiler_params=pltpu.CompilerParams(vmem_limit_bytes=limit * MIB),
        cost_estimate=pl.CostEstimate(
            flops=int(us * 8e8), bytes_accessed=int(us * 1e5), transcendentals=0
        ),
        name=name,
    )(*args)


def array(*shape, dtype=BF16):
    return jax.ShapeDtypeStruct(shape, dtype)


def first_query(me, p, b):
    z, y, c = me // 4, (me // 2) % 2, me % 2
    (z0, y0), (z1, y1) = SOURCE[p]
    z = lax.rem(z + NZ + z0 + c * (z1 - z0), NZ)
    y = lax.rem(y + NY + y0 + c * (y1 - y0), NY)
    core = lax.rem(c + b + (p in (2, 4, 6)), 2)
    return pl.multiple_of((z * 4 + y * 2 + core) * ROWS, ROWS)


def piece_at(dp, n):
    half, dx, dy = n // 8, DP_STEPS[n % 8 // 2], n % 2
    return (lax.rem(dp // NX + dy, NYH) * NX + lax.rem(dp % NX + dx, NX)) * 2 + half


def encode_kernel(x_ref, gain_ref, w_in_hbm, w_out_hbm, out_ref, w_in_ref, w_out_ref, sems):
    parts = [slice(i * FTILE, (i + 1) * FTILE) for i in range(FF // FTILE)]
    copies = []
    for i, part in enumerate(parts):
        into = pltpu.make_async_copy(w_in_hbm.at[:, part], w_in_ref.at[:, part], sems.at[0, i])
        out = pltpu.make_async_copy(w_out_hbm.at[part, :], w_out_ref.at[part, :], sems.at[1, i])
        into.start()
        out.start()
        copies.append((into, out))
    values = x_ref[...].astype(F32)
    meansq = jnp.mean(values * values, axis=-1, keepdims=True)
    normed = (values * lax.rsqrt(meansq + 1e-06) * gain_ref[...].reshape(1, D)).astype(BF16)
    total = values
    for part, (into, out) in zip(parts, copies):
        into.wait()
        active = jax.nn.gelu(
            jnp.dot(normed, w_in_ref[:, part], preferred_element_type=F32), approximate=True
        ).astype(BF16)
        out.wait()
        total = total + jnp.dot(active, w_out_ref[part, :], preferred_element_type=F32)
    out_ref[...] = total.astype(BF16)


def encode(hidden_in, norm_gain, w_in, w_out):
    return pl.pallas_call(
        encode_kernel,
        out_shape=array(ROWS, D),
        in_specs=[VMEM, VMEM, HBM, HBM],
        out_specs=VMEM,
        scratch_shapes=[
            pltpu.VMEM((D, FF), BF16),
            pltpu.VMEM((FF, D), BF16),
            pltpu.SemaphoreType.DMA((2, FF // FTILE)),
        ],
        compiler_params=pltpu.CompilerParams(vmem_limit_bytes=60 * MIB),
        cost_estimate=pl.CostEstimate(
            flops=int(4e9), bytes_accessed=int(1e7), transcendentals=0
        ),
        name="encode",
    )(hidden_in, norm_gain, w_in, w_out)


def prepare(me, dp, sl_ref, pos_ref, bs_ref, base_ref, wa_ref, wb_ref):
    slot_rows = lax.broadcasted_iota(jnp.int32, (LBLK, BLOCKS), 0)
    place, piece = slot_rows // PIECE_SLOTS, jnp.zeros_like(slot_rows)
    for n in range(LOCAL // PIECE):
        piece = jnp.where(place == n, piece_at(dp, n), piece)
    slot_rows = slot_rows % PIECE_SLOTS + piece * PIECE_SLOTS + me * LBLK
    ids = lax.broadcasted_iota(jnp.int32, (LBLK, BLOCKS), 1).astype(F32)
    here = jnp.sum(jnp.where(bs_ref[...] == slot_rows, ids, 0.0), axis=1, keepdims=True)
    here = jnp.broadcast_to(here, (LBLK, ROWS))
    which = lax.broadcasted_iota(jnp.int32, (K, ROWS), 0)
    for p in range(PAIRS):
        for b in range(2):
            lanes = pl.ds(first_query(me, p, b), ROWS)
            sl = sl_ref[:, lanes].astype(F32)
            pos = pos_ref[:, lanes]
            base = jnp.zeros((LBLK, ROWS), F32)
            for k in range(K):
                base = jnp.where(here == sl[k : k + 1], 0.5, base)
            wa = jnp.zeros((LBLK, ROWS), jnp.int32)
            wb = jnp.zeros((LBLK, ROWS), jnp.int32)
            for n in range(P_SIZE):
                kp, jp = pos[n : n + 1] >> 6, pos[n : n + 1] & 63
                bid = jnp.sum(jnp.where(which == kp, sl, 0.0), axis=0, keepdims=True)
                bit = jnp.full((1, ROWS), 1, jnp.int32) << (31 - (jp & 31))
                match = here == bid
                wa = wa | jnp.where(match, jnp.where(jp < 32, bit, 0), 0)
                wb = wb | jnp.where(match, jnp.where(jp < 32, 0, bit), 0)
            out = slice(b * ROWS, (b + 1) * ROWS)
            base_ref[p, :, out] = base
            wa_ref[p, :, out] = wa
            wb_ref[p, :, out] = wb


def loss_rows(row):
    hi = row.astype(BF16)
    rest = row - hi.astype(F32)
    mid = rest.astype(BF16)
    lo = (rest - mid.astype(F32)).astype(BF16)
    return jnp.concatenate([hi, mid, lo, jnp.zeros((EXTRA, D - 3 * ROWS), BF16)], axis=1)


def joined(rows):
    return rows[:, :ROWS] + rows[:, ROWS : 2 * ROWS] + rows[:, 2 * ROWS : 3 * ROWS]


def add_pair(a_ref, b_ref, out_ref):
    for b in [()] if len(out_ref.shape) == 2 else [(0,), (1,)]:
        grad, loss = b + (slice(0, ROWS),), b + (slice(ROWS, ROWS + EXTRA),)
        out_ref[grad] = (a_ref[grad].astype(F32) + b_ref[grad].astype(F32)).astype(BF16)
        out_ref[loss] = loss_rows(joined(a_ref[loss].astype(F32) + b_ref[loss].astype(F32)))


def slopes(numbers, at, tiles, q_ref, c_ref, flags, s_ref, x_refs, wait, done):
    base_ref, wa_ref, wb_ref = flags
    steps = [(j, i) for j in range(len(numbers)) for i in tiles]
    shift = lax.broadcasted_iota(jnp.int32, (32, ROWS), 0)

    def logits(n):
        j, i = steps[n]
        wait(j, i)
        j += at
        i -= c_ref.shape[0] < LOCAL and tiles[0]
        x_refs[n % 2][...] = lax.dot_general(
            c_ref[i * TILE : (i + 1) * TILE, :],
            q_ref[j * PAIR : (j + 1) * PAIR, :],
            (((1,), (1,)), ((), ())),
            preferred_element_type=F32,
        )

    logits(0)
    for k, (j, i) in enumerate(steps):
        p = numbers[j]
        if k + 1 < len(steps):
            logits(k + 1)
        if i == tiles[0]:
            slot = slice(tiles[0] * SLOTS, (tiles[-1] + 1) * SLOTS)
            count = 2.0 * jnp.sum(base_ref[p, slot, :], axis=0, keepdims=True)
            losses = [
                jnp.broadcast_to((LN2 * BL / 8) * count[:, t * ROWS : (t + 1) * ROWS], (8, ROWS))
                for t in range(2)
            ]
        for t in range(2):
            lanes = slice(t * ROWS, (t + 1) * ROWS)
            into = slice((at + j) * PAIR + t * ROWS, (at + j) * PAIR + (t + 1) * ROWS)
            prod = jnp.ones((8, ROWS), F32)
            relu = jnp.zeros((8, ROWS), F32)
            for n in range(TILE // BL):
                slot = slice(i * (TILE // BL) + n, i * (TILE // BL) + n + 1)
                rows = slice(i * TILE + n * BL, i * TILE + (n + 1) * BL)
                base = base_ref[p, slot, lanes]
                bits = jnp.concatenate(
                    [wa_ref[p, slot, lanes] << shift, wb_ref[p, slot, lanes] << shift], axis=0
                )
                half = jnp.where(bits < 0, -base, base)
                y = x_refs[k % 2][n * BL : (n + 1) * BL, lanes] * half
                th = jnp.tanh(y)
                s_ref[rows, into] = (half * th + half).astype(BF16)
                u8 = (1.0 + jnp.abs(th)).reshape(BL // 8, 8, ROWS)
                r8 = jnp.maximum(y, 0.0).reshape(BL // 8, 8, ROWS)
                for m in range(BL // 8):
                    prod = prod * u8[m]
                    relu = relu + r8[m]
            losses[t] = losses[t] + (2.0 * relu - jnp.log(prod))
        if i == tiles[-1]:
            done(j, jnp.sum(jnp.concatenate(losses, axis=1), axis=0, keepdims=True))


PART = array(2, ROWS + EXTRA, D)
HALF_PART = array(ROWS + EXTRA, D)
NEAR, REST = (0, 7), (1, 2, 3, 4, 5, 6)
FAR_Q = len(NEAR) * PAIR
FLAGS = tuple(array(PAIRS, LBLK, PAIR, dtype=t) for t in (F32, jnp.int32, jnp.int32))
X_SCRATCH = [pltpu.VMEM((TILE, PAIR), F32)] * 2
CLASS_ROWS = LOCAL // (NX * NYH)


def query_part(s_ref, j, c_ref, loss, outs):
    total = lax.dot_general(
        s_ref[:, j * PAIR : (j + 1) * PAIR],
        c_ref[...],
        (((0,), (0,)), ((), ())),
        preferred_element_type=F32,
    )
    for b, out in enumerate(outs):
        out[:ROWS, :] = total[b * ROWS : (b + 1) * ROWS].astype(BF16)
        row = jnp.broadcast_to(loss[:, b * ROWS : (b + 1) * ROWS], (EXTRA, ROWS))
        out[ROWS:, :] = loss_rows(row)


class Copies:
    def __init__(self, sems):
        self.sems, self.count = sems, 0

    def start(self, source, target):
        copy = pltpu.make_async_copy(source, target, self.sems.at[self.count])
        copy.start()
        self.count += 1
        return copy


def fill(copies, sources, q_ref, row):
    started = []
    for source in sources:
        rows = source.shape[0]
        started.append(copies.start(source, q_ref.at[row : row + rows, :]))
        row += rows
    return started


def label_copies(copies, dp_ref, c_hbm, c_ref, tiles):
    started = []
    for n, i in enumerate(tiles):
        both = []
        for b in range(2):
            at = piece_at(dp_ref[0], 2 * i + b)
            rows = pl.ds(pl.multiple_of(at * PIECE, PIECE), PIECE)
            into = slice(n * TILE + b * PIECE, n * TILE + (b + 1) * PIECE)
            both.append(copies.start(c_hbm.at[rows, :], c_ref.at[into, :]))
        started.append(both)
    return started


def wait_all(copies):
    for copy in copies:
        copy.wait()


def near_kernel(me_ref, dp_ref, sl_ref, pos_ref, bs_ref, c_hbm, own, other, far, far2,
                s_hbm, part0, keep7, give7, base_ref, wa_ref, wb_ref,
                c_ref, q_ref, s_ref, x0_ref, x1_ref, sems):
    copies = Copies(sems)
    queries = fill(copies, (own, other), q_ref, 0)
    labels = label_copies(copies, dp_ref, c_hbm, c_ref, range(TILES))
    queries += fill(copies, (far, far2), q_ref, PAIR)
    prepare(me_ref[0], dp_ref[0], sl_ref, pos_ref, bs_ref, base_ref, wa_ref, wb_ref)
    outs = ((part0.at[0], part0.at[1]), (keep7, give7))
    stored = []

    def wait(j, i):
        if i == 0:
            queries[2 * j].wait()
            queries[2 * j + 1].wait()
        if j == 0:
            wait_all(labels[i])

    def done(j, loss):
        columns = slice(j * PAIR, (j + 1) * PAIR)
        stored.append(copies.start(s_ref.at[:, columns], s_hbm.at[:, columns]))
        query_part(s_ref, j, c_ref, loss, outs[j])

    slopes(NEAR, 0, range(TILES), q_ref, c_ref, (base_ref, wa_ref, wb_ref), s_ref, (x0_ref, x1_ref), wait, done)
    for copy in stored:
        copy.wait()


def gate_kernel(dep_ref, *refs):
    del dep_ref, refs


def gate(dep, *arrays):
    return pl.pallas_call(
        gate_kernel,
        out_shape=tuple(array(*a.shape) for a in arrays),
        in_specs=[ANY] * (1 + len(arrays)),
        out_specs=(ANY,) * len(arrays),
        input_output_aliases={n + 1: n for n in range(len(arrays))},
        cost_estimate=pl.CostEstimate(flops=1000, bytes_accessed=1000, transcendentals=0),
        name="gate",
    )(dep, *arrays)


REST_Q = len(REST) * PAIR


def class_part(s_ref, row, q_ref, blocks):
    for n in range(0, len(blocks), 2):
        at = row + n * TILE
        total = jnp.dot(s_ref[at : at + 2 * TILE, :], q_ref[...], preferred_element_type=F32)
        blocks[n][...] = total[:TILE].astype(BF16)
        blocks[n + 1][...] = total[TILE:].astype(BF16)


def first_kernel(dp_ref, base_hbm, wa_hbm, wb_hbm, c_hbm, s_near, *refs):
    n = len(PIECES)
    pieces, (s_hbm, loss_ref), blocks = refs[:n], refs[n : n + 2], refs[n + 2 : n + 6]
    base_ref, wa_ref, wb_ref, c_ref, q_ref, s_ref, x0_ref, x1_ref, sems = refs[n + 6 :]
    copies = Copies(sems)
    flags = [
        copies.start(source, target)
        for source, target in ((base_hbm, base_ref), (wa_hbm, wa_ref), (wb_hbm, wb_ref))
    ]
    queries = fill(copies, pieces[4:5], q_ref, FAR_Q)
    labels = label_copies(copies, dp_ref, c_hbm, c_ref, range(TILES // 2))
    queries += fill(copies, pieces[5:], q_ref, FAR_Q + PAIR)
    early = fill(copies, pieces[:4], q_ref, 0)
    early.append(copies.start(s_near.at[:HALF, :], s_ref.at[:, :FAR_Q]))
    stored = []
    for copy in flags:
        copy.wait()

    def wait(j, i):
        if i == 0:
            queries[j].wait()
        if j == 0:
            wait_all(labels[i])

    def done(j, loss):
        at = slice(FAR_Q + j * PAIR, FAR_Q + (j + 1) * PAIR)
        columns = slice(j * PAIR, (j + 1) * PAIR)
        stored.append(copies.start(s_ref.at[:, at], s_hbm.at[:, columns]))
        loss_ref[:, columns] = loss

    slopes(REST, len(NEAR), range(TILES // 2), q_ref, c_ref, (base_ref, wa_ref, wb_ref), s_ref,
           (x0_ref, x1_ref), wait, done)
    for copy in early:
        copy.wait()
    class_part(s_ref, 0, q_ref, blocks)
    for copy in stored:
        copy.wait()


def second_kernel(dp_ref, loss_ref, base_hbm, wa_hbm, wb_hbm, c_hbm, s_near, s_first, *refs):
    n, m = len(PIECES), len(PIECES) + len(REST)
    pieces, parts, blocks = refs[:n], refs[n:m], refs[m : m + 4]
    base_ref, wa_ref, wb_ref, c_ref, q_ref, s_ref, x0_ref, x1_ref, sems = refs[m + 4 :]
    copies = Copies(sems)
    flags = [
        copies.start(source, target)
        for source, target in ((base_hbm, base_ref), (wa_hbm, wa_ref), (wb_hbm, wb_ref))
    ]
    queries = fill(copies, pieces[4:5], q_ref, FAR_Q)
    half = range(TILES // 2, TILES)
    labels = label_copies(copies, dp_ref, c_hbm, c_ref.at[HALF:, :], half)
    queries += fill(copies, pieces[5:], q_ref, FAR_Q + PAIR)
    before = [copies.start(s_first, s_ref.at[:HALF, FAR_Q:])]
    before += sum(label_copies(copies, dp_ref, c_hbm, c_ref, range(TILES // 2)), [])
    early = fill(copies, pieces[:4], q_ref, 0)
    early.append(copies.start(s_near.at[HALF:, :], s_ref.at[HALF:, :FAR_Q]))
    for copy in flags:
        copy.wait()

    def wait(j, i):
        if i == half[0]:
            queries[j].wait()
        if j == 0:
            wait_all(labels[i - half[0]])

    def done(j, loss):
        if j == 0:
            for copy in before:
                copy.wait()
        loss = loss + loss_ref[:, j * PAIR : (j + 1) * PAIR]
        query_part(s_ref, len(NEAR) + j, c_ref, loss, (parts[j].at[0], parts[j].at[1]))

    slopes(REST, len(NEAR), half, q_ref, c_ref, (base_ref, wa_ref, wb_ref), s_ref,
           (x0_ref, x1_ref), wait, done)
    for copy in early:
        copy.wait()
    class_part(s_ref, HALF, q_ref, blocks)


def sum_kernel(count, *refs):
    for n in range(count):
        add_pair(refs[2 * n], refs[2 * n + 1], refs[len(refs) - count + n])


def along_x_kernel(own, a, b, c, keep, give):
    total = sum(r[...].astype(F32) for r in (own, a, b, c))
    keep[...] = total[:PIECE]
    give[...] = total[PIECE:].astype(BF16)


def along_x(blocks):
    *sent, own = blocks
    moved = [
        lax.ppermute(block, "dp", dp_perm(dx, 0)) for dx, block in zip(DP_STEPS, sent)
    ]
    return call(
        along_x_kernel,
        "along_x",
        1,
        (array(PIECE, D, dtype=F32), array(PIECE, D)),
        [VMEM] * 4,
        (own, *moved),
    )


def along_y_kernel(keep0, r0, keep1, r1, out):
    for half, (keep, r) in enumerate(((keep0, r0), (keep1, r1))):
        out[half * PIECE : (half + 1) * PIECE, :] = (keep[...] + r[...].astype(F32)).astype(BF16)


def collect_kernel(own, a, b, d, keep, give):
    keep[...] = sum(r[0].astype(F32) for r in (own, a, b, d))
    total = sum(r[1].astype(F32) for r in (own, a, b, d))
    give[:ROWS, :] = total[:ROWS].astype(BF16)
    give[ROWS:, :] = loss_rows(joined(total[ROWS:]))


def finish_kernel(keep, other, far, grad_ref, loss_ref):
    total = keep[...] + other[...].astype(F32) + far[...].astype(F32)
    grad_ref[...] = total[:ROWS].astype(BF16)
    loss_ref[...] = joined(total[ROWS : ROWS + 8])[:1]


PIECES = ((0, 0), (0, 1), (7, 0), (7, 1)) + tuple((p, 0) for p in REST)


def bound_kernel(me_ref, every_ref, *refs):
    q_refs, (_, out_ref, cent_ref, radii_ref) = refs[: len(PIECES)], refs[len(PIECES) :]
    me = me_ref[0]
    for n in range(BLOCKS // LBLK):
        rows = slice(n * LBLK, (n + 1) * LBLK)
        cent_ref[rows, :] = every_ref[n, :LBLK, :D]
        terms = every_ref[n, :LBLK, D:].astype(F32)
        radius = terms[:, 0:1] + terms[:, 1:2] + terms[:, 2:3]
        radii_ref[rows, :] = jnp.broadcast_to(radius, (LBLK, ROWS))
    ones = jnp.ones((8, D), BF16)
    over_row = lambda a, b: lax.dot_general(
        a, b, (((1,), (1,)), ((), ())), preferred_element_type=F32
    )
    for (p, half), q in zip(PIECES, q_refs):
        value = q[...].astype(F32)
        square = value * value
        high = square.astype(BF16)
        low = (square - high.astype(F32)).astype(BF16)
        norm = jnp.sqrt(over_row(ones, high) + over_row(ones, low))[:1]
        score = over_row(cent_ref[...], q[...])
        for b in range(q.shape[0] // ROWS):
            lanes = slice(b * ROWS, (b + 1) * ROWS)
            bound = score[:, lanes] + radii_ref[...] * norm[:, lanes]
            out_ref[:, pl.ds(first_query(me, p, half + b), ROWS)] = jnp.max(
                bound, axis=0, keepdims=True
            )


def after(value, *others):
    return lax.optimization_barrier((value, others))[0]


def on_device(
    hidden_in,
    norm_gain,
    w_in,
    w_out,
    classifier,
    centroids,
    radii,
    shortlist,
    positives,
    block_slot,
):
    label = lax.axis_index("label")
    dp = lax.axis_index("dp")
    me = label.astype(jnp.int32).reshape(1)

    hi = lax.reduce_precision(radii, 8, 7)
    mid = lax.reduce_precision(radii - hi, 8, 7)
    lo = lax.reduce_precision(radii - hi - mid, 8, 7)
    terms = jnp.stack([hi, mid, lo], axis=1).astype(BF16)
    packed = jnp.concatenate([centroids, jnp.pad(terms, ((0, 0), (0, CWIDTH - D - 3)))], axis=1)
    every = lax.all_gather(jnp.pad(packed, ((0, CROWS - LBLK), (0, 0))), "label", axis=0)

    encoded = encode(hidden_in, norm_gain, w_in, w_out)

    far = from_source(encoded, 7)
    other = swap(encoded)
    pair = jnp.concatenate([encoded, other])
    near = (encoded, other, far, swap(far))
    dp = dp.astype(jnp.int32).reshape(1)
    s_near, part0, keep7, give7, *flags = call(
        near_kernel,
        "near",
        0.5,
        (array(LOCAL, FAR_Q), PART, HALF_PART, HALF_PART) + FLAGS,
        [SMEM] * 2 + [VMEM] * 3 + [ANY] * 5,
        (me, dp, shortlist.T, positives.T, block_slot.reshape(1, -1), classifier, *near),
        [
            pltpu.VMEM((LOCAL, D), BF16),
            pltpu.VMEM((FAR_Q, D), BF16),
            pltpu.VMEM((LOCAL, FAR_Q), BF16),
            *X_SCRATCH,
            pltpu.SemaphoreType.DMA((4 + 2 * TILES + 2,)),
        ],
        out_specs=(ANY,) + (VMEM,) * 6,
    )
    received = gate(keep7, *(from_source(pair, p) for p in (1, 3, 5)))
    rest = tuple(r for q in received for r in (q, swap(q)))
    pieces = near + rest
    flag_scratch = [pltpu.VMEM(f.shape, f.dtype) for f in FLAGS]
    s_first, loss_first, *first = call(
        first_kernel,
        "first_half",
        12,
        (array(HALF, REST_Q), array(1, REST_Q, dtype=F32)) + (array(TILE, D),) * 4,
        [SMEM] + [ANY] * (5 + len(pieces)),
        (dp, *flags, classifier, s_near, *pieces),
        flag_scratch
        + [
            pltpu.VMEM((HALF, D), BF16),
            pltpu.VMEM((PAIRS * PAIR, D), BF16),
            pltpu.VMEM((HALF, PAIRS * PAIR), BF16),
            *X_SCRATCH,
            pltpu.SemaphoreType.DMA((3 + len(pieces) + TILES + 1 + len(REST),)),
        ],
        out_specs=(ANY,) + (VMEM,) * 5,
    )
    *parts, = call(
        second_kernel,
        "second_half",
        18,
        (PART,) * len(REST) + (array(TILE, D),) * 4,
        [SMEM, VMEM] + [ANY] * (6 + len(pieces)),
        (dp, loss_first, *flags, classifier, s_near, s_first, *pieces),
        flag_scratch
        + [
            pltpu.VMEM((LOCAL, D), BF16),
            pltpu.VMEM((PAIRS * PAIR, D), BF16),
            pltpu.VMEM((LOCAL, PAIRS * PAIR), BF16),
            *X_SCRATCH,
            pltpu.SemaphoreType.DMA((3 + len(pieces) + 2 * TILES + 2,)),
        ],
    )
    keep_first, give_first = along_x(first)
    keep_second, give_second = along_x(parts[len(REST) :])

    bound_top = call(
        bound_kernel,
        "bounds",
        6,
        array(1, PAIRS * PAIR, dtype=F32),
        [SMEM] + [VMEM] * (len(PIECES) + 1) + [ANY],
        (me, every, *pieces, give_first),
        [pltpu.VMEM((BLOCKS, D), BF16), pltpu.VMEM((BLOCKS, ROWS), F32)],
    )
    sum1, sum3, sum5, sum7 = call(
        functools.partial(sum_kernel, 4),
        "sums",
        2,
        (PART, PART, PART, HALF_PART),
        [VMEM] * 8 + [ANY],
        (
            *(t for n in (0, 2, 4) for t in (parts[n], swap(parts[n + 1]))),
            keep7,
            swap(give7),
            bound_top,
        ),
    )
    far_part = to_source(sum7, 7)
    keep, give = call(
        collect_kernel,
        "collect",
        1,
        (array(ROWS + EXTRA, D, dtype=F32), HALF_PART),
        [VMEM] * 4,
        (part0, to_source(sum1, 1), to_source(sum3, 3), to_source(sum5, 5)),
    )
    query_grad, loss = call(
        finish_kernel,
        "finish",
        1,
        (array(ROWS, D), array(1, ROWS, dtype=F32)),
        [VMEM] * 3,
        (keep, swap(give), far_part),
    )
    class_grad = call(
        along_y_kernel,
        "along_y",
        1,
        array(2 * PIECE, D),
        [VMEM] * 4,
        (
            keep_first,
            lax.ppermute(give_first, "dp", dp_perm(0, 1)),
            keep_second,
            lax.ppermute(give_second, "dp", dp_perm(0, 1)),
        ),
    )
    return bound_top.reshape(-1), loss.reshape(-1), query_grad, class_grad


def solution(mesh):
    placed = (
        P(("dp", "label"), None),
        P(),
        P(),
        P(),
        P("label", None),
        P("label", None),
        P("label"),
        P("dp", None),
        P("dp", None),
        P(),
    )
    return jax.shard_map(
        on_device,
        mesh=mesh,
        in_specs=placed,
        out_specs=(P("dp"), P(("dp", "label")), P(("dp", "label"), None), P(("label", "dp"), None)),
        check_vma=False,
    )
```
